256 devices in a mesh: lat: 8 (over x, y_lo), lon: 32 (over z, y_hi, core).
Axes of the slice: x: 4, y: 4 (y_hi: 2, y_lo: 2; y = y_hi * 2 + y_lo), z: 8, core: 2. Of those that a mesh axis runs over, the one named last changes fastest.
Arguments:
- cells: bfloat16 [192, 768, 512], P('lat', 'lon'), may hold values from -6 to 6
- cotangent: bfloat16 [192, 768, 512], P('lat', 'lon'), may hold values from -3 to 3
- land: int32 [192, 768], P('lat', 'lon'), may hold values 0 or 1
- land_embed: float32 [512], replicated, may hold values from -3 to 3
- qkv_weight: bfloat16 [512, 1536], P('lon')
- proj_weight: bfloat16 [512, 512], P('lon'), may hold values from -0.25 to 0.25
- up_weight: bfloat16 [512, 2048], P('lon'), may hold values from -0.25 to 0.25
- down_weight: bfloat16 [2048, 512], P('lon'), may hold values from -0.125 to 0.125
- gain_one: bfloat16 [512], P('lon'), may hold values from 0.5 to 1.5
- gain_two: bfloat16 [512], P('lon'), may hold values from 0.5 to 1.5
Outputs:
- block_out: bfloat16 [192, 768, 512], P('lat', 'lon')
- grad_cells: bfloat16 [192, 768, 512], P('lat', 'lon')
- grad_qkv: float32 [512, 1536], P('lon')
- grad_proj: float32 [512, 512], P('lon')
- grad_up: float32 [512, 2048], P('lon')
- grad_down: float32 [2048, 512], P('lon')
- grad_gain_one: float32 [512], P('lon')
- grad_gain_two: float32 [512], P('lon')
The draws below stay inside these ranges and needn't reach their ends.
All inputs are finite; a program needn't handle non-finite values. No bound on the sum of `land` on one device may be relied on, other than what follows from the above.
Results may differ from the reference program's by a relative error of at most 0.04.
The reference program's roundings to bfloat16 on the way count: a program that leaves them out, or rounds other values in their place, can miss the bound.
Values may be sent and summed in bfloat16 or wider, within the bound.
A program may use at most 128 MiB of HBM per device.

```python
import jax
import jax.numpy as jnp
from jax import lax

D = 512
HEADS = 16
HID = 2048
WIN = 12
SHIFT = 6
LAT_CELLS = 192
LON_CELLS = 768


def draw_qkv_weight(key, part):
    key = jax.random.fold_in(key, 7)
    first = jax.random.fold_in(key, 0)
    base = jax.random.normal(first, (D, 3 * D), jnp.float32) * D ** (-0.5)
    return base.astype(jnp.bfloat16)


def set_ends(array, key, smallest, largest):
    longest = array.shape.index(max(array.shape))
    spots = []
    for shift in (0, 1):
        where = [jax.random.randint(jax.random.fold_in(key, axis), (), 0, length) for axis, length in enumerate(array.shape)]
        where[longest] = (where[longest] + shift) % array.shape[longest]
        spots.append(tuple(where))
    return array.at[spots[0]].set(smallest).at[spots[1]].set(largest)


def steps_of(rng, dims, pieces, smallest, high):
    level, own = 1.0, jax.random.fold_in(rng, 6)
    for dim, shards_of in pieces:
        steps = jnp.exp(jax.random.uniform(jax.random.fold_in(own, dim), (shards_of,), jnp.float32, smallest / len(pieces), high / len(pieces)))
        level = level * jnp.repeat(steps, dims[dim] // shards_of).reshape([-1 if axis == dim else 1 for axis in range(len(dims))])
    return level


def bell_draw(stream_key, shape, scale, most, pieces=(), kind=jnp.bfloat16):
    result = scale * jax.random.normal(stream_key, shape, jnp.float32)
    if pieces:
        result = result * steps_of(stream_key, shape, pieces, -0.22, 0.18)
    return jnp.clip(result, -most, most).astype(kind)


def setup_inputs(seed: int = 0) -> dict:
    streams_of = jax.random.split(jax.random.key(seed), 11)
    cells = bell_draw(streams_of[0], (LAT_CELLS, LON_CELLS, D), 1.0, 6.0, ((0, 8), (1, 32)))
    cotangent = bell_draw(streams_of[1], (LAT_CELLS, LON_CELLS, D), 0.5, 3.0, ((0, 8), (1, 32)))
    land = set_ends((jax.random.randint(streams_of[2], (LAT_CELLS, LON_CELLS), 0, 3) < 1).astype(jnp.int32), jax.random.fold_in(streams_of[2], 1), 0, 1)
    land_embed = bell_draw(streams_of[3], (D,), 0.5, 3.0, (), jnp.float32)
    qkv_weight = draw_qkv_weight(jax.random.fold_in(streams_of[10], 71), 0)
    proj_weight = bell_draw(streams_of[5], (D, D), D ** -0.5, 0.25, ((0, 32),))
    up_weight = bell_draw(streams_of[6], (D, HID), D ** -0.5, 0.25, ((0, 32),))
    down_weight = bell_draw(streams_of[7], (HID, D), HID ** -0.5, 0.125, ((0, 32),))
    gain_one = jnp.clip(1.0 + 0.1 * jax.random.normal(streams_of[8], (D,), jnp.float32), 0.5, 1.5).astype(jnp.bfloat16)
    gain_two = jnp.clip(1.0 + 0.1 * jax.random.normal(streams_of[9], (D,), jnp.float32), 0.5, 1.5).astype(jnp.bfloat16)
    return {"cells": cells, "cotangent": cotangent, "land": land, "land_embed": land_embed, "qkv_weight": qkv_weight, "proj_weight": proj_weight, "up_weight": up_weight, "down_weight": down_weight, "gain_one": gain_one, "gain_two": gain_two}


epsilon = 1e-05
negative = -1e+30

def float_einsum(form, left, right):
    return jnp.einsum(form, left.astype(jnp.float32), right.astype(jnp.float32))

def left_product(left, right):
    return jnp.dot(left.T, right, preferred_element_type=jnp.float32)

def right_product(left, right):
    return jnp.dot(left, right.T, preferred_element_type=jnp.float32)

def take_columns(values, start, count):
    return lax.dynamic_slice_in_dim(values, start, count, 1)

def take_rows(values, start, count):
    return lax.dynamic_slice_in_dim(values, start, count, 0)

def layer_norm(values, gain):
    center = lax.optimization_barrier(jnp.mean(values, axis=-1, keepdims=True))
    centred = values - center
    spread = lax.optimization_barrier(jnp.mean(centred * centred, axis=-1, keepdims=True))
    inverse = lax.rsqrt(spread + epsilon)
    normed = centred * inverse
    return (normed, inverse, (normed * gain).astype(jnp.bfloat16))

def norm_back(upstream, normed, inverse, gain):
    scaled = upstream * gain
    inner = scaled - lax.optimization_barrier(jnp.mean(scaled, axis=-1, keepdims=True)) - normed * lax.optimization_barrier(jnp.mean(scaled * normed, axis=-1, keepdims=True))
    return (inner * inverse, lax.optimization_barrier(jnp.sum(upstream * normed, axis=0)))

def windowed(field):
    height, breadth, depth = field.shape
    shaped = field.reshape(height // WIN, WIN, breadth // WIN, WIN, depth)
    return shaped.transpose(0, 2, 1, 3, 4).reshape(height * breadth, depth)

def unwindow(tokens, height, breadth):
    depth = tokens.shape[1]
    shaped = tokens.reshape(height // WIN, breadth // WIN, WIN, WIN, depth)
    return shaped.transpose(0, 2, 1, 3, 4).reshape(height, breadth, depth)

def gelu_slope(values):
    return 0.5 * (1.0 + lax.erf(values * 0.7071067811865476)) + values * jnp.exp(-0.5 * values * values) * 0.3989422804014327

def block_pass(field, upstream, rows_global, limit, weights, settle, refetch):
    height, breadth, width = field.shape
    head_size = width // HEADS
    scale = head_size ** (-0.5)
    tokens = windowed(field)
    count_tokens = tokens.shape[0]
    groups = count_tokens // (WIN * WIN)
    flags = jnp.broadcast_to((rows_global >= limit).astype(jnp.int32)[:, None, None], (height, breadth, 1))
    region = windowed(flags).reshape(groups, WIN * WIN)
    qkv_weight, proj_weight, up_weight, down_weight, gain_one, gain_two = weights
    inputs = tokens.astype(jnp.float32)
    normed_one, inverse_one, hidden_one = layer_norm(inputs, gain_one.astype(jnp.float32))
    packed = jnp.dot(hidden_one, qkv_weight, preferred_element_type=jnp.float32).astype(jnp.bfloat16)
    split = packed.reshape(groups, WIN * WIN, 3, HEADS, head_size)
    query = split[:, :, 0]
    keyed = split[:, :, 1]
    valued = split[:, :, 2]
    scores = float_einsum('wqhd,wkhd->whqk', query, keyed) * scale
    allowed = region[:, None, :, None] == region[:, None, None, :]
    scores = jnp.where(allowed, scores, negative)
    highest = lax.optimization_barrier(jnp.max(scores, axis=-1, keepdims=True))
    raised = jnp.exp(scores - highest)
    probs = raised / lax.optimization_barrier(jnp.sum(raised, axis=-1, keepdims=True))
    probs_low = probs.astype(jnp.bfloat16)
    attended = float_einsum('whqk,wkhd->wqhd', probs_low, valued).astype(jnp.bfloat16).reshape(count_tokens, width)
    middle = inputs + jnp.dot(attended, proj_weight, preferred_element_type=jnp.float32)
    normed_two, inverse_two, hidden_two = layer_norm(middle, gain_two.astype(jnp.float32))
    raised_up = jnp.dot(hidden_two, up_weight, preferred_element_type=jnp.float32)
    active = jax.nn.gelu(raised_up, approximate=False).astype(jnp.bfloat16)
    output = (middle + jnp.dot(active, down_weight, preferred_element_type=jnp.float32)).astype(jnp.bfloat16)
    qkv_back, proj_back, up_back, down_back, gain_one_back, gain_two_back = refetch(weights)
    incoming = windowed(upstream)
    grad_down = settle(lambda start, count: left_product(take_columns(active, start, count), incoming), active.shape[1])
    grad_active = right_product(incoming, down_back)
    grad_raised = (grad_active * gelu_slope(raised_up)).astype(jnp.bfloat16)
    grad_up = settle(lambda start, count: left_product(take_columns(hidden_two, start, count), grad_raised), width)
    grad_hidden_two = right_product(grad_raised, up_back)
    grad_middle_norm, gain_two_sum = norm_back(grad_hidden_two, normed_two, inverse_two, gain_two_back.astype(jnp.float32))
    grad_gain_two = settle(lambda start, count: take_rows(gain_two_sum, start, count), width)
    grad_middle = incoming.astype(jnp.float32) + grad_middle_norm
    grad_middle_low = grad_middle.astype(jnp.bfloat16)
    grad_proj = settle(lambda start, count: left_product(take_columns(attended, start, count), grad_middle_low), width)
    grad_attended = right_product(grad_middle_low, proj_back).astype(jnp.bfloat16).reshape(groups, WIN * WIN, HEADS, head_size)
    grad_probs = float_einsum('wqhd,wkhd->whqk', grad_attended, valued)
    grad_valued = float_einsum('whqk,wqhd->wkhd', probs_low, grad_attended)
    grad_scores = probs * (grad_probs - lax.optimization_barrier(jnp.sum(grad_probs * probs, axis=-1, keepdims=True))) * scale
    grad_scores_low = grad_scores.astype(jnp.bfloat16)
    grad_query = float_einsum('whqk,wkhd->wqhd', grad_scores_low, keyed)
    grad_keyed = float_einsum('whqk,wqhd->wkhd', grad_scores_low, query)
    grad_packed = jnp.stack([grad_query, grad_keyed, grad_valued], axis=2).reshape(count_tokens, 3 * width).astype(jnp.bfloat16)
    grad_qkv = settle(lambda start, count: left_product(take_columns(hidden_one, start, count), grad_packed), width)
    grad_hidden_one = right_product(grad_packed, qkv_back)
    grad_inputs_norm, gain_one_sum = norm_back(grad_hidden_one, normed_one, inverse_one, gain_one_back.astype(jnp.float32))
    grad_gain_one = settle(lambda start, count: take_rows(gain_one_sum, start, count), width)
    grad_inputs = (grad_middle + grad_inputs_norm).astype(jnp.bfloat16)
    grads = (grad_qkv, grad_proj, grad_up, grad_down, grad_gain_one, grad_gain_two)
    return (unwindow(output, height, breadth), unwindow(grad_inputs, height, breadth), grads)

def plain_settle(function, total):
    return function(0, total)

def same_weights(weights):
    return weights

def reference(cells, cotangent, land, land_embed, qkv_weight, proj_weight, up_weight, down_weight, gain_one, gain_two):
    start = (cells.astype(jnp.float32) + land[:, :, None].astype(jnp.float32) * land_embed[None, None, :]).astype(jnp.bfloat16)
    moved = jnp.roll(start, (-SHIFT, -SHIFT), (0, 1))
    moved_cot = jnp.roll(cotangent, (-SHIFT, -SHIFT), (0, 1))
    strips = LAT_CELLS // WIN
    moved = moved.reshape(strips, WIN, LON_CELLS, D)
    moved_cot = moved_cot.reshape(strips, WIN, LON_CELLS, D)
    weights = (qkv_weight, proj_weight, up_weight, down_weight, gain_one, gain_two)
    initial = tuple((jnp.zeros(item.shape, jnp.float32) for item in weights))

    def advance(carry, item):
        field, upstream, index = item
        rows_global = index * WIN + jnp.arange(WIN, dtype=jnp.int32)
        output, grad_inputs, grads = block_pass(field, upstream, rows_global, LAT_CELLS - SHIFT, weights, plain_settle, same_weights)
        return (tuple((total + part for total, part in zip(carry, grads))), (output, grad_inputs))
    totals, (outputs, grad_inputs) = lax.scan(advance, initial, (moved, moved_cot, jnp.arange(strips, dtype=jnp.int32)))
    block_out = jnp.roll(outputs.reshape(LAT_CELLS, LON_CELLS, D), (SHIFT, SHIFT), (0, 1))
    grad_cells = jnp.roll(grad_inputs.reshape(LAT_CELLS, LON_CELLS, D), (SHIFT, SHIFT), (0, 1))
    return (block_out, grad_cells, totals[0], totals[1], totals[2], totals[3], totals[4], totals[5])
```

```python
import functools

import jax
import jax.numpy as jnp
from jax import lax
from jax.experimental import pallas as pl
from jax.experimental.pallas import tpu as pltpu
from jax.sharding import PartitionSpec as P

HEADS = 16
WIN = 12
SHIFT = 6
EPS = 1e-5
NEG = -1e30
TOK = WIN * WIN
QUAD = SHIFT * SHIFT
PADQ = 48
GROUP = 256
F32 = jnp.float32
BF16 = jnp.bfloat16
MESH = pl.DeviceIdType.MESH


def nn(a, b):
    return lax.dot_general(a, b, (((1,), (0,)), ((), ())), preferred_element_type=F32)


def nt(a, b):
    return lax.dot_general(a, b, (((1,), (1,)), ((), ())), preferred_element_type=F32)


def tn(a, b):
    return lax.dot_general(a, b, (((0,), (0,)), ((), ())), preferred_element_type=F32)


def layer_norm(x):
    centred = x - jnp.mean(x, axis=-1, keepdims=True)
    spread = jnp.mean(centred * centred, axis=-1, keepdims=True)
    inverse = lax.rsqrt(spread + EPS)
    return centred * inverse, inverse


def norm_back(upstream, normed, inverse, gain):
    scaled = upstream * gain
    inner = (
        scaled
        - jnp.mean(scaled, axis=-1, keepdims=True)
        - normed * jnp.mean(scaled * normed, axis=-1, keepdims=True)
    )
    return inner * inverse, jnp.sum(upstream * normed, axis=0, keepdims=True)


class Place:
    def __init__(self, lats, lons):
        self.lats, self.lons, self.rings = lats, lons, lons // 4
        self.lat = lax.axis_index("lat")
        self.lon = lax.axis_index("lon")
        self.z = self.lon // 4
        self.yh = (self.lon // 2) % 2
        self.core = self.lon % 2
        self.sibling = (self.lat, self.lon + 1 - 2 * self.core)
        near = self.lat + 1 - 2 * (self.lat % 2)
        self.partner = (near, self.z * 4 + (1 - self.yh) * 2 + self.core)

    def along_z(self, by):
        z = (self.z + by + self.rings) % self.rings
        return (self.lat, z * 4 + self.yh * 2 + self.core)

    def moved(self, by_lat, by_lon):
        lat = (self.lat + by_lat + self.lats) % self.lats
        lon = (self.lon + by_lon + self.lons) % self.lons
        return (lat, lon)

    def in_plane(self, by):
        index = (self.yh * self.lats + self.lat + by) % (2 * self.lats)
        return index // self.lats, index % self.lats

    def plane_device(self, by):
        yh, lat = self.in_plane(by)
        return (lat, self.z * 4 + yh * 2 + self.core)


class Wires:
    def __init__(self, send, recv):
        self.send, self.recv, self.used, self.sent = send, recv, 0, []

    def take(self, count):
        first = self.used
        self.used += count
        return first

    def copy(self, src, dst, index, device):
        return pltpu.make_async_remote_copy(
            src_ref=src,
            dst_ref=dst,
            send_sem=self.send.at[index],
            recv_sem=self.recv.at[index],
            device_id=device,
            device_id_type=MESH,
        )

    def start(self, src, dst, index, device, until=None):
        self.copy(src, dst, index, device).start()
        if until is not None:
            self.sent.append((until, index))

    def landed(self, ref, index, device):
        self.copy(ref, ref, index, device).wait_recv()

    def finish(self, device):
        for view, index in self.sent:
            ref = view()
            self.copy(ref, ref, index, device).wait_send()


class Gather:
    def __init__(self, place, wires, shard, whole):
        self.p, self.w, self.shard, self.whole = place, wires, shard, whole
        self.right, self.left = place.rings // 2, place.rings // 2 - 1
        self.base = wires.take(1 + self.right + self.left + place.rings)

    def slot(self, rel, core):
        p = self.p
        return self.whole.at[(p.z - rel + p.rings) % p.rings, :, core]

    def begin(self):
        p = self.p
        here = self.whole.at[p.z, p.yh, p.core]
        here[...] = self.shard[...]
        self.w.start(self.shard, here, self.base, p.partner, lambda: self.shard)

    def share(self, rel):
        p = self.p
        index = self.base + 1 + self.right + self.left + rel
        block = self.slot(rel, p.core)
        self.w.start(block, block, index, p.sibling, lambda: self.whole.at[0, :, 0])

    def tick(self, step):
        p = self.p
        if step == 0:
            self.w.landed(self.whole.at[p.z, 1 - p.yh, p.core], self.base, p.partner)
            arrived = (0,)
        else:
            arrived = []
            self.w.landed(self.slot(step, p.core), self.base + step, p.along_z(-1))
            arrived.append(step)
            if step <= self.left:
                index = self.base + self.right + step
                self.w.landed(self.slot(p.rings - step, p.core), index, p.along_z(1))
                arrived.append(p.rings - step)
        if step < self.right:
            block = self.slot(step, p.core)
            index = self.base + 1 + step
            self.w.start(block, block, index, p.along_z(1), lambda: self.whole.at[0, :, 0])
        if step < self.left:
            block = self.slot((p.rings - step) % p.rings, p.core)
            index = self.base + 1 + self.right + step
            self.w.start(block, block, index, p.along_z(-1), lambda: self.whole.at[0, :, 0])
        for rel in arrived:
            self.share(rel)

    def end(self):
        p = self.p
        for rel in range(p.rings):
            index = self.base + 1 + self.right + self.left + rel
            self.w.landed(self.slot(rel, 1 - p.core), index, p.sibling)


class Scatter:
    def __init__(self, place, wires, refs, cut, pieces):
        self.p, self.w, self.cut, self.pieces = place, wires, cut, pieces
        self.own, self.away, self.near, self.out, self.into, self.stage, self.land, self.full = refs
        self.right, self.left = place.rings // 2, place.rings // 2 - 1
        self.exchange = wires.take(pieces)
        self.ring = wires.take(self.right + self.left)
        self.plane = wires.take(2 * place.lats - 1)
        self.along = wires.take(place.lats - 1)

    def put(self, part, value):
        where, _ = self.cut(part)
        first, second = value[..., 0, :, :], value[..., 1, :, :]
        mine = self.p.core == 0
        self.own[where] = jnp.where(mine, first, second)
        self.away[where] = jnp.where(mine, second, first).astype(BF16)

    def trade(self, part):
        where, index = self.cut(part)
        self.w.copy(
            self.away.at[where], self.near.at[where], self.exchange + index, self.p.sibling
        ).start()

    def traded(self, part):
        where, index = self.cut(part)
        copy = self.w.copy(
            self.away.at[where], self.near.at[where], self.exchange + index, self.p.sibling
        )
        copy.wait_send()
        copy.wait_recv()

    def share(self, rel):
        p = self.p
        z = (p.z + rel + p.rings) % p.rings
        return self.own[z] + self.near[z].astype(F32)

    def tick(self, step):
        p = self.p
        total = self.share(self.right + 1 - step)
        if step > 1:
            before = step - 2
            self.w.landed(self.into.at[before], self.ring + before, p.along_z(-1))
            total = total + self.into[before].astype(F32)
        self.out[step - 1] = total.astype(BF16)
        source = self.out.at[step - 1]
        self.w.start(
            source, self.into.at[step - 1], self.ring + step - 1, p.along_z(1), lambda: self.out.at[0]
        )
        if step <= self.left:
            slot = self.right + step - 1
            total = self.share(-(self.left + 1 - step))
            if step > 1:
                self.w.landed(self.into.at[slot - 1], self.ring + slot - 1, p.along_z(1))
                total = total + self.into[slot - 1].astype(F32)
            self.out[slot] = total.astype(BF16)
            source = self.out.at[slot]
            self.w.start(source, self.into.at[slot], self.ring + slot, p.along_z(-1), lambda: self.out.at[0])

    def spread(self, divide):
        p = self.p
        total = self.share(0)
        slots = [(self.right - 1, -1)]
        if self.left:
            slots.append((self.right + self.left - 1, 1))
        for slot, by in slots:
            self.w.landed(self.into.at[slot], self.ring + slot, p.along_z(by))
            total = total + self.into[slot].astype(F32)
        for yh in range(2):
            for sub in range(p.lats):
                self.stage[yh, sub] = divide(total[yh], sub)
        for by in range(1, 2 * p.lats):
            yh, lat = p.in_plane(by)
            self.w.start(
                self.stage.at[yh, lat],
                self.land.at[by - 1],
                self.plane + by - 1,
                p.plane_device(by),
                lambda: self.land.at[0],
            )

    def collect(self):
        p = self.p
        total = self.stage[p.yh, p.lat]
        for by in range(1, 2 * p.lats):
            self.w.landed(
                self.land.at[by - 1], self.plane + by - 1, p.plane_device(2 * p.lats - by)
            )
            total = total + self.land[by - 1]
        self.full[p.lat] = total
        block = self.full.at[p.lat]
        for by in range(1, p.lats):
            self.w.start(block, block, self.along + by - 1, p.moved(by, 0), lambda: self.full.at[0])

    def end(self):
        p = self.p
        for by in range(1, p.lats):
            lat = (p.lat - by + p.lats) % p.lats
            self.w.landed(self.full.at[lat], self.along + by - 1, (lat, p.lon))


def shifted_blocks():
    for window in range(4):
        for quarter in range(4):
            i = 2 * (window // 2) + quarter // 2
            j = 2 * (window % 2) + quarter % 2
            yield i, j, window, quarter, i == 3, j == 3


def kernel(
    lats,
    lons,
    field,
    shard_one,
    shard_two,
    shard_three,
    out_field,
    out_one,
    out_two,
    out_three,
    moved,
    back,
    x_ref,
    up_ref,
    low_up,
    hidden_one,
    packed,
    probs_ref,
    attended,
    middle,
    result,
    hidden_two,
    active,
    grad_raised,
    grad_attended,
    grad_low,
    grad_packed,
    gains,
    sums,
    one,
    two,
    three,
    *rest,
):
    scatter_refs, (send_sem, recv_sem) = rest[:-2], rest[-2:]
    p = Place(lats, lons)
    wires = Wires(send_sem, recv_sem)
    width = x_ref.shape[1]
    hid = shard_two.shape[1]
    chunk = hid // p.rings
    rows = width // lons
    tokens = 4 * TOK
    scale = (width // HEADS) ** -0.5
    per = GROUP * HEADS // width
    head = width // HEADS
    groups = width // GROUP

    barrier = pltpu.get_barrier_semaphore()
    friends = [p.plane_device(by) for by in range(1, 2 * lats)]
    friends += [p.sibling, p.along_z(1), p.along_z(-1)]
    friends += [p.moved(0, 1), p.moved(0, -1), p.moved(1, 1), p.moved(-1, -1)]
    for friend in friends:
        pl.semaphore_signal(barrier, inc=1, device_id=friend, device_id_type=MESH)
    pl.semaphore_wait(barrier, len(friends))

    def beyond(by_rows, by_columns, sign):
        return p.moved(sign * int(by_rows), sign * int(by_columns))

    halo = wires.take(7)
    edge = [item for item in shifted_blocks() if item[4] or item[5]]
    gathers = [
        Gather(p, wires, shard, whole)
        for shard, whole in ((shard_one, one), (shard_two, two), (shard_three, three))
    ]
    gathers[0].begin()
    for number, (i, j, window, quarter, down, over) in enumerate(edge):
        wires.start(
            field.at[(i + 1) % 4, (j + 1) % 4],
            moved.at[window, quarter],
            halo + number,
            beyond(down, over, -1),
            lambda: moved.at[0, 0],
        )
    gathers[0].tick(0)
    gathers[1].begin()
    gathers[2].begin()
    for step in range(1, gathers[0].right + 1):
        gathers[0].tick(step)

    for number, (i, j, window, quarter, down, over) in enumerate(edge):
        wires.landed(moved.at[window, quarter], halo + number, beyond(down, over, 1))
    for i, j, window, quarter, down, over in shifted_blocks():
        source = moved.at[window, quarter] if down or over else field.at[i + 1, j + 1]
        first = TOK * window + QUAD * quarter
        x_ref[pl.ds(first, PADQ)] = source[0].astype(F32)
        up_ref[pl.ds(first, PADQ)] = source[1].astype(F32)

    gathers[0].end()
    pending = [
        functools.partial(gather.tick, step)
        for gather in gathers[1:]
        for step in range(gather.right + 1)
    ]

    def weight(ref, first, count):
        return ref[:, :, :, :, pl.ds(first, count)].reshape(width, count)

    turned = jnp.transpose(weight(one, 4 * width, 128).astype(F32), (1, 0))
    gains[0:8] = jnp.broadcast_to(turned[0:1], (8, width))
    gains[8:16] = jnp.broadcast_to(turned[64:65], (8, width))

    def by_rows(body):
        def run(window, _):
            body(pl.ds(pl.multiple_of(window * TOK, 16), TOK))
            return 0

        lax.fori_loop(0, 4, run, 0)

    def first_norm(at):
        normed, _ = layer_norm(x_ref[at])
        hidden_one[at] = (normed * gains[0:1]).astype(BF16)
        low_up[at] = up_ref[at].astype(BF16)

    by_rows(first_norm)

    def columns(count, body):
        def run(number, _):
            body(pl.multiple_of(number * GROUP, GROUP), number)
            return 0

        lax.fori_loop(0, count, run, 0)

    def pack(first, number):
        packed[:, pl.ds(first, GROUP)] = nn(hidden_one[...], weight(one, first, GROUP)).astype(
            BF16
        )

    columns(3 * groups, pack)

    lanes = lax.broadcasted_iota(jnp.int32, (TOK, GROUP), 1) // head
    late = lax.broadcasted_iota(jnp.int32, (TOK, TOK), 0) >= TOK // 2
    late_query = lax.broadcasted_iota(jnp.int32, (TOK, TOK), 1) >= TOK // 2
    differ = late != late_query

    def head_lanes(first):
        return pl.ds(pl.multiple_of(first, GROUP), GROUP)

    def attend(number, _):
        window, group = number // groups, number % groups
        at = pl.ds(pl.multiple_of(window * TOK, 16), TOK)
        query = packed[at, head_lanes(group * GROUP)]
        keyed = packed[at, head_lanes(width + group * GROUP)]
        valued = packed[at, head_lanes(2 * width + group * GROUP)]
        split = jnp.logical_and(p.lat == lats - 1, window >= 2)
        bias = jnp.where(jnp.logical_and(differ, split), NEG, 0.0)
        value_turned = jnp.transpose(valued.astype(F32), (1, 0)).astype(BF16)
        parts = []
        for h in range(per):
            mine = jnp.where(lanes == h, keyed, jnp.zeros_like(keyed))
            scores = nt(mine, query) * scale + bias
            raised = jnp.exp(scores - jnp.max(scores, axis=0, keepdims=True))
            probs = raised * (1.0 / jnp.sum(raised, axis=0, keepdims=True))
            probs_ref[number * per + h] = probs
            parts.append(nn(value_turned[h * head : (h + 1) * head], probs.astype(BF16)))
        attended[at, head_lanes(group * GROUP)] = jnp.transpose(
            jnp.concatenate(parts, axis=0), (1, 0)
        ).astype(BF16)
        for turn, action in enumerate(pending[: 4 * groups]):
            pl.when(number == turn)(action)
        return 0

    lax.fori_loop(0, 4 * groups, attend, 0)
    for action in pending[4 * groups :]:
        action()

    def project(first, number):
        middle[:, pl.ds(first, GROUP)] = x_ref[0:tokens, pl.ds(first, GROUP)] + nn(
            attended[...], weight(one, pl.multiple_of(3 * width + first, GROUP), GROUP)
        )

    columns(groups, project)

    def second_norm(at):
        normed, _ = layer_norm(middle[at])
        hidden_two[at] = (normed * gains[8:9]).astype(BF16)

    by_rows(second_norm)
    gathers[1].end()
    gathers[2].end()

    sizes = (4 * width + 128, hid, width)
    whole_rows = (rows, rows, chunk // 4)

    def by_columns(part):
        return (slice(None), slice(None), slice(None), pl.ds(part * GROUP, GROUP)), part

    def by_hidden(part):
        first = pl.multiple_of(part * chunk, 128)
        return (slice(None), slice(None), slice(None), pl.ds(first, chunk)), part

    def whole(part):
        return (slice(None), slice(None), slice(None), slice(None)), part

    def by_ring(part):
        return (part,), part

    scatters = [
        Scatter(p, wires, scatter_refs[8 * k : 8 * k + 8], cut, pieces)
        for k, (cut, pieces) in enumerate(((whole, 1), (by_hidden, p.rings), (by_ring, p.rings)))
    ]

    def feed(number, _):
        first = pl.ds(pl.multiple_of(number * chunk, 128), chunk)
        up_weight = two[:, :, :, :, first].reshape(width, chunk)
        raised_up = nn(hidden_two[...], up_weight)
        share = 0.5 * (1.0 + lax.erf(raised_up * 0.7071067811865476))
        act = (raised_up * share).astype(BF16)
        active[:, first] = act
        slope = share + raised_up * jnp.exp(-0.5 * raised_up * raised_up) * 0.3989422804014327
        grad_down = tn(act, low_up[...])
        scatters[2].put(number, grad_down.reshape(2, 2, chunk // 4, width))
        scatters[2].trade(number)
        down_weight = three[number].reshape(chunk, width)
        grads = (nt(low_up[...], down_weight) * slope).astype(BF16)
        grad_raised[:, first] = grads
        grad_up = tn(hidden_two[...], grads)
        scatters[1].put(number, grad_up.reshape(p.rings, 2, 2, rows, chunk))
        scatters[1].trade(number)
        return 0

    lax.fori_loop(0, p.rings, feed, 0)

    def wait_trades(scatter):
        def run(number, _):
            scatter.traded(number)
            return 0

        lax.fori_loop(0, scatter.pieces, run, 0)

    wait_trades(scatters[2])
    scatters[2].tick(1)

    def lower(first, number):
        down = three[:, :, :, :, pl.ds(first, GROUP)].reshape(hid, GROUP)
        result[0:tokens, pl.ds(first, GROUP)] = middle[:, pl.ds(first, GROUP)] + nn(
            active[...], down
        )

    columns(groups, lower)

    returns = wires.take(14)

    def send_back(source, kind):
        number = 0
        for i, j, window, quarter, down, over in shifted_blocks():
            first = TOK * window + QUAD * quarter
            block = source[pl.ds(first, PADQ)].astype(BF16)
            target = out_field.at[(i + 1) % 4, (j + 1) % 4, kind]
            if down or over:
                place = back.at[number, kind]
                place[...] = block
                index = returns + 7 * kind + number
                wires.start(place, target, index, beyond(down, over, 1), lambda: back.at[0, 0])
                number += 1
            else:
                target[...] = block

    send_back(result, 0)
    wait_trades(scatters[1])
    scatters[2].tick(2)
    scatters[1].tick(1)

    def raise_back(first, number):
        share = p.rings // groups
        up_rows = two[pl.ds(number * share, share)].reshape(GROUP, hid)
        result[0:tokens, pl.ds(first, GROUP)] = nt(grad_raised[...], up_rows)

    columns(groups, raise_back)
    scatters[2].tick(3)
    scatters[1].tick(2)

    sums[...] = jnp.zeros_like(sums)

    def second_back(at):
        normed, inverse = layer_norm(middle[at])
        through, total = norm_back(result[at], normed, inverse, gains[8:9])
        sums[8:16] += jnp.broadcast_to(total, (8, width))
        grad_middle = up_ref[at] + through
        up_ref[at] = grad_middle
        grad_low[at] = grad_middle.astype(BF16)

    by_rows(second_back)
    scatters[2].tick(4)
    scatters[1].tick(3)

    def split_columns(value):
        return value.reshape(p.rings, 2, 2, rows, value.shape[1])

    def project_back(first, number):
        grad = tn(attended[...], grad_low[:, pl.ds(first, GROUP)])
        scatters[0].put_at(
            pl.ds(pl.multiple_of(3 * width + first, GROUP), GROUP), split_columns(grad)
        )
        share = p.rings // groups
        proj_rows = one[pl.ds(number * share, share), :, :, :, pl.ds(3 * width, width)]
        grad_attended[:, pl.ds(first, GROUP)] = nt(
            grad_low[...], proj_rows.reshape(GROUP, width)
        ).astype(BF16)

    columns(groups, project_back)
    scatters[2].spread(lambda total, sub: total[sub * (chunk // 4 // lats) : (sub + 1) * (chunk // 4 // lats)])
    scatters[1].tick(4)

    later = [
        scatters[2].collect,
        functools.partial(
            scatters[1].spread,
            lambda total, sub: total[:, sub * (hid // lats) : (sub + 1) * (hid // lats)],
        ),
        scatters[2].end,
        scatters[1].collect,
        scatters[1].end,
    ]

    def attend_back(number, _):
        window, group = number // groups, number % groups
        at = pl.ds(pl.multiple_of(window * TOK, 16), TOK)
        query = packed[at, head_lanes(group * GROUP)]
        keyed = packed[at, head_lanes(width + group * GROUP)]
        valued = packed[at, head_lanes(2 * width + group * GROUP)]
        upstream = grad_attended[at, head_lanes(group * GROUP)]
        key_turned = jnp.transpose(keyed.astype(F32), (1, 0)).astype(BF16)
        grad_key = jnp.zeros((TOK, GROUP), F32)
        grad_value = jnp.zeros((TOK, GROUP), F32)
        parts = []
        for h in range(per):
            probs = probs_ref[number * per + h]
            mine = lanes == h
            grad_probs = nt(jnp.where(mine, valued, jnp.zeros_like(valued)), upstream)
            grad_value = jnp.where(mine, nn(probs.astype(BF16), upstream), grad_value)
            inner = jnp.sum(grad_probs * probs, axis=0, keepdims=True)
            grad_scores = (probs * (grad_probs - inner) * scale).astype(BF16)
            grad_key = jnp.where(mine, nn(grad_scores, query), grad_key)
            parts.append(nn(key_turned[h * head : (h + 1) * head], grad_scores))
        grad_query = jnp.transpose(jnp.concatenate(parts, axis=0), (1, 0))
        grad_packed[at, head_lanes(group * GROUP)] = grad_query.astype(BF16)
        grad_packed[at, head_lanes(width + group * GROUP)] = grad_key.astype(BF16)
        grad_packed[at, head_lanes(2 * width + group * GROUP)] = grad_value.astype(BF16)
        for turn, action in enumerate(later):
            pl.when(number == turn)(action)
        return 0

    lax.fori_loop(0, 4 * groups, attend_back, 0)

    def pack_back(first, number):
        grad = tn(hidden_one[...], grad_packed[:, pl.ds(first, GROUP)])
        scatters[0].put_at(pl.ds(first, GROUP), split_columns(grad))

    columns(3 * groups, pack_back)

    def unpack(first, number):
        share = p.rings // groups
        rows_here = one[pl.ds(number * share, share), :, :, :, pl.ds(0, 3 * width)]
        result[0:tokens, pl.ds(first, GROUP)] = nt(
            grad_packed[...], rows_here.reshape(GROUP, 3 * width)
        )

    columns(groups, unpack)

    def first_back(at):
        normed, inverse = layer_norm(x_ref[at])
        through, total = norm_back(result[at], normed, inverse, gains[0:1])
        sums[0:8] += jnp.broadcast_to(total, (8, width))
        up_ref[at] = up_ref[at] + through

    by_rows(first_back)
    line = lax.broadcasted_iota(jnp.int32, (128, width), 0)
    both = jnp.where(line < 64, sums[0:1], sums[8:9])
    scatters[0].put_at(pl.ds(4 * width, 128), split_columns(jnp.transpose(both, (1, 0))))
    scatters[0].trade(0)
    send_back(up_ref, 1)
    scatters[0].traded(0)
    for step in range(1, scatters[0].right + 1):
        scatters[0].tick(step)
    share = 4 * width // lats
    scatters[0].spread(
        lambda total, sub: jnp.concatenate(
            [total[:, sub * share : (sub + 1) * share], total[:, 4 * width :]], axis=1
        )
    )
    scatters[0].collect()
    scatters[0].end()
    for sub in range(lats):
        out_three[sub * (chunk // 4 // lats) : (sub + 1) * (chunk // 4 // lats)] = scatters[2].full[
            sub
        ]
        out_two[:, sub * (hid // lats) : (sub + 1) * (hid // lats)] = scatters[1].full[sub]
        out_one[:, sub * share : (sub + 1) * share] = scatters[0].full[sub, :, 0:share]
    out_one[:, 4 * width :] = scatters[0].full[0, :, share:]
    number = 0
    for i, j, window, quarter, down, over in shifted_blocks():
        if down or over:
            for kind in range(2):
                wires.landed(
                    out_field.at[(i + 1) % 4, (j + 1) % 4, kind],
                    returns + 7 * kind + number,
                    beyond(down, over, -1),
                )
            number += 1
    wires.finish(p.sibling)


def put_at(self, columns, value):
    first, second = value[..., 0, :, :], value[..., 1, :, :]
    mine = self.p.core == 0
    self.own[:, :, :, columns] = jnp.where(mine, first, second)
    self.away[:, :, :, columns] = jnp.where(mine, second, first).astype(BF16)


Scatter.put_at = put_at


def blocks_of(field):
    height, breadth, depth = field.shape
    shaped = field.reshape(height // SHIFT, SHIFT, breadth // SHIFT, SHIFT, depth)
    shaped = shaped.transpose(0, 2, 1, 3, 4).reshape(4, 4, QUAD, depth)
    return jnp.pad(shaped, ((0, 0), (0, 0), (0, PADQ - QUAD), (0, 0)))


def field_of(blocks):
    depth = blocks.shape[-1]
    shaped = blocks[:, :, :QUAD].reshape(4, 4, SHIFT, SHIFT, depth)
    return shaped.transpose(0, 2, 1, 3, 4).reshape(4 * SHIFT, 4 * SHIFT, depth)


def body(
    lats,
    lons,
    cells,
    cotangent,
    land,
    land_embed,
    qkv_weight,
    proj_weight,
    up_weight,
    down_weight,
    gain_one,
    gain_two,
):
    start = (
        cells.astype(F32) + land[:, :, None].astype(F32) * land_embed[None, None, :]
    ).astype(BF16)
    field = jnp.stack([blocks_of(start), blocks_of(cotangent)], axis=2)
    rows, hid = up_weight.shape
    width = cells.shape[2]
    deep = down_weight.shape[0]
    tokens = 4 * TOK
    rings = lons // 4
    shard_one = jnp.concatenate(
        [
            qkv_weight,
            proj_weight,
            jnp.broadcast_to(gain_one[:, None], (rows, 64)),
            jnp.broadcast_to(gain_two[:, None], (rows, 64)),
        ],
        axis=1,
    )
    wide = 4 * width + 128

    def scatter_scratch(lines, across, piece):
        return [
            pltpu.VMEM((rings, 2, lines, across), F32),
            pltpu.VMEM((rings, 2, lines, across), BF16),
            pltpu.VMEM((rings, 2, lines, across), BF16),
            pltpu.VMEM((rings - 1, 2, lines, across), BF16),
            pltpu.VMEM((rings - 1, 2, lines, across), BF16),
            pltpu.VMEM((2, lats) + piece, F32),
            pltpu.VMEM((2 * lats - 1,) + piece, F32),
            pltpu.VMEM((lats,) + piece, F32),
        ]

    scratch = [
        pltpu.VMEM((4, 4, 2, PADQ, width), BF16),
        pltpu.VMEM((7, 2, PADQ, width), BF16),
        pltpu.VMEM((tokens + 16, width), F32),
        pltpu.VMEM((tokens + 16, width), F32),
        pltpu.VMEM((tokens, width), BF16),
        pltpu.VMEM((tokens, width), BF16),
        pltpu.VMEM((tokens, 3 * width), BF16),
        pltpu.VMEM((4 * HEADS, TOK, TOK), F32),
        pltpu.VMEM((tokens, width), BF16),
        pltpu.VMEM((tokens, width), F32),
        pltpu.VMEM((tokens + 16, width), F32),
        pltpu.VMEM((tokens, width), BF16),
        pltpu.VMEM((tokens, hid), BF16),
        pltpu.VMEM((tokens, hid), BF16),
        pltpu.VMEM((tokens, width), BF16),
        pltpu.VMEM((tokens, width), BF16),
        pltpu.VMEM((tokens, 3 * width), BF16),
        pltpu.VMEM((16, width), F32),
        pltpu.VMEM((16, width), F32),
        pltpu.VMEM((rings, 2, 2, rows, wide), BF16),
        pltpu.VMEM((rings, 2, 2, rows, hid), BF16),
        pltpu.VMEM((rings, 2, 2, deep, width), BF16),
    ]
    scratch += scatter_scratch(rows, wide, (rows, 4 * width // lats + 128))
    scratch += scatter_scratch(rows, hid, (rows, hid // lats))
    scratch += scatter_scratch(deep, width, (deep // lats, width))
    wires = 7 + 14 + 3 * (2 * rings)
    wires += (1 + rings - 1 + 3 * lats - 2) + 2 * (rings + rings - 1 + 3 * lats - 2)
    scratch += [pltpu.SemaphoreType.DMA((wires,)), pltpu.SemaphoreType.DMA((wires,))]
    vmem = pl.BlockSpec(memory_space=pltpu.VMEM)
    out_field, one, two, three = pl.pallas_call(
        functools.partial(kernel, lats, lons),
        out_shape=(
            jax.ShapeDtypeStruct((4, 4, 2, PADQ, width), BF16),
            jax.ShapeDtypeStruct((rows, wide), F32),
            jax.ShapeDtypeStruct((rows, hid), F32),
            jax.ShapeDtypeStruct((deep, width), F32),
        ),
        in_specs=[vmem] * 4,
        out_specs=(vmem,) * 4,
        scratch_shapes=scratch,
        compiler_params=pltpu.CompilerParams(
            collective_id=0, has_side_effects=True, vmem_limit_bytes=63 * 2**20
        ),
        name="block",
    )(field, shard_one, up_weight, down_weight)
    return (
        field_of(out_field[:, :, 0]),
        field_of(out_field[:, :, 1]),
        one[:, : 3 * width],
        one[:, 3 * width : 4 * width],
        two,
        three,
        one[:, 4 * width],
        one[:, 4 * width + 64],
    )


def solution(mesh):
    placed = (
        P("lat", "lon", None),
        P("lat", "lon", None),
        P("lat", "lon"),
        P(),
        P("lon", None),
        P("lon", None),
        P("lon", None),
        P("lon", None),
        P("lon"),
        P("lon"),
    )
    return jax.shard_map(
        functools.partial(body, mesh.shape["lat"], mesh.shape["lon"]),
        mesh=mesh,
        in_specs=placed,
        out_specs=(
            P("lat", "lon", None),
            P("lat", "lon", None),
            P("lon", None),
            P("lon", None),
            P("lon", None),
            P("lon", None),
            P("lon"),
            P("lon"),
        ),
        check_vma=False,
    )
```

```python
import functools

import jax
import jax.numpy as jnp
from jax import lax
from jax.experimental import pallas as pl
from jax.experimental.pallas import tpu as pltpu
from jax.sharding import PartitionSpec as P

HEADS = 16
WIN = 12
SHIFT = 6
EPS = 1e-5
NEG = -1e30
TOK = WIN * WIN
QUAD = SHIFT * SHIFT
PADQ = 48
GROUP = 256
F32 = jnp.float32
BF16 = jnp.bfloat16
MESH = pl.DeviceIdType.MESH


def nn(a, b):
    return lax.dot_general(a, b, (((1,), (0,)), ((), ())), preferred_element_type=F32)


def nt(a, b):
    return lax.dot_general(a, b, (((1,), (1,)), ((), ())), preferred_element_type=F32)


def tn(a, b):
    return lax.dot_general(a, b, (((0,), (0,)), ((), ())), preferred_element_type=F32)


def layer_norm(x):
    centred = x - jnp.mean(x, axis=-1, keepdims=True)
    spread = jnp.mean(centred * centred, axis=-1, keepdims=True)
    inverse = lax.rsqrt(spread + EPS)
    return centred * inverse, inverse


def norm_back(upstream, normed, inverse, gain):
    scaled = upstream * gain
    inner = (
        scaled
        - jnp.mean(scaled, axis=-1, keepdims=True)
        - normed * jnp.mean(scaled * normed, axis=-1, keepdims=True)
    )
    return inner * inverse, jnp.sum(upstream * normed, axis=0, keepdims=True)


class Marks:
    def __init__(self):
        self.open = None

    def __call__(self, name=None):
        if self.open is not None:
            self.open.__exit__(None, None, None)
        self.open = None
        if name is not None:
            self.open = jax.named_scope(name)
            self.open.__enter__()


class Place:
    def __init__(self, lats, lons):
        self.lats, self.lons, self.rings = lats, lons, lons // 4
        self.lat = lax.axis_index("lat")
        self.lon = lax.axis_index("lon")
        self.z = self.lon // 4
        self.yh = (self.lon // 2) % 2
        self.core = self.lon % 2
        self.sibling = (self.lat, self.lon + 1 - 2 * self.core)
        near = self.lat + 1 - 2 * (self.lat % 2)
        self.partner = (near, self.z * 4 + (1 - self.yh) * 2 + self.core)

    def along_z(self, by):
        z = (self.z + by + self.rings) % self.rings
        return (self.lat, z * 4 + self.yh * 2 + self.core)

    def moved(self, by_lat, by_lon):
        lat = (self.lat + by_lat + self.lats) % self.lats
        lon = (self.lon + by_lon + self.lons) % self.lons
        return (lat, lon)

    def in_plane(self, by):
        index = (self.yh * self.lats + self.lat + by) % (2 * self.lats)
        return index // self.lats, index % self.lats

    def plane_device(self, by):
        yh, lat = self.in_plane(by)
        return (lat, self.z * 4 + yh * 2 + self.core)


class Wires:
    def __init__(self, send, recv):
        self.send, self.recv, self.used, self.sent = send, recv, 0, []

    def take(self, count):
        first = self.used
        self.used += count
        return first

    def copy(self, src, dst, index, device):
        return pltpu.make_async_remote_copy(
            src_ref=src,
            dst_ref=dst,
            send_sem=self.send.at[index],
            recv_sem=self.recv.at[index],
            device_id=device,
            device_id_type=MESH,
        )

    def start(self, src, dst, index, device, until=None):
        self.copy(src, dst, index, device).start()
        if until is not None:
            self.sent.append((until, index))

    def landed(self, ref, index, device):
        self.copy(ref, ref, index, device).wait_recv()

    def finish(self, device):
        for view, index in self.sent:
            ref = view()
            self.copy(ref, ref, index, device).wait_send()


class Gather:
    def __init__(self, place, wires, shard, whole):
        self.p, self.w, self.shard, self.whole = place, wires, shard, whole
        self.half = place.rings // 2
        self.last = 2 * self.half
        self.far = wires.take(1)
        self.way = {1: wires.take(self.last - 1), -1: wires.take(self.last - 1)}
        self.side = wires.take(place.rings)

    def slot(self, rel, other):
        p = self.p
        yh = 1 - p.yh if other else p.yh
        return self.whole.at[(p.z - rel + p.rings) % p.rings, yh, p.core]

    def pair(self, rel, core):
        p = self.p
        return self.whole.at[(p.z - rel + p.rings) % p.rings, :, core]

    def forward(self, way, hop, other):
        if hop == self.half - 1 and other != (way < 0):
            return
        index = self.way[way] + (2 * hop + other if hop < self.half - 1 else 2 * hop)
        block = self.slot(way * hop, other)
        self.w.start(block, block, index, self.p.along_z(way), lambda: self.whole.at[0, 0, 0])

    def landed(self, way, hop, other):
        index = self.way[way] + (2 * (hop - 1) + other if hop < self.half else 2 * (hop - 1))
        self.w.landed(self.slot(way * hop, other), index, self.p.along_z(-way))

    def share(self, rel):
        p = self.p
        index = self.side + rel % p.rings
        block = self.pair(rel, p.core)
        self.w.start(block, block, index, p.sibling, lambda: self.whole.at[0, :, 0])

    def tick(self, step):
        p = self.p
        if step == 0:
            here = self.slot(0, 0)
            here[...] = self.shard[...]
            for way in (1, -1):
                self.forward(way, 0, 0)
            self.w.start(self.shard, here, self.far, p.partner, lambda: self.shard)
        elif step == 1:
            self.w.landed(self.slot(0, 1), self.far, p.partner)
            for way in (1, -1):
                self.forward(way, 0, 1)
            self.share(0)
        elif step < self.last:
            hop, other = step // 2, step % 2
            for way in (1, -1):
                self.landed(way, hop, other)
                self.forward(way, hop, other)
            if other:
                for way in (1, -1):
                    self.share(way * hop)
        else:
            self.landed(1, self.half, 0)
            self.landed(-1, self.half, 1)
            self.share(self.half)

    def end(self):
        p = self.p
        for rel in range(p.rings):
            self.w.landed(self.pair(rel, 1 - p.core), self.side + rel, p.sibling)


class Scatter:
    def __init__(self, place, wires, refs, pieces):
        self.p, self.w, self.pieces = place, wires, pieces
        self.own, self.away, self.near, self.out, self.into, self.stage, self.land, self.full = refs
        self.half = place.rings // 2
        self.last = 2 * self.half - 1
        self.exchange = wires.take(pieces)
        self.ring = wires.take(2 * self.last)
        self.plane = wires.take(2 * place.lats - 1)
        self.along = wires.take(place.lats - 1)
        self.lines = self.own.shape[2] // place.lats

    def put(self, where, value):
        first, second = value[..., 0, :, :], value[..., 1, :, :]
        mine = self.p.core == 0
        self.own[where] = jnp.where(mine, first, second)
        self.away[where] = jnp.where(mine, second, first).astype(BF16)

    def trade(self, where, index):
        self.w.copy(
            self.away.at[where], self.near.at[where], self.exchange + index, self.p.sibling
        ).start()

    def traded(self, where, index):
        copy = self.w.copy(
            self.away.at[where], self.near.at[where], self.exchange + index, self.p.sibling
        )
        copy.wait_send()
        copy.wait_recv()

    def share(self, rel, yh):
        p = self.p
        z = (p.z + rel + p.rings) % p.rings
        return self.own[z, yh] + self.near[z, yh].astype(F32)

    def pass_on(self, way, rel, yh):
        p = self.p
        base = 0 if way > 0 else self.last
        slot = base + 2 * rel - 2 + yh if rel < self.half else base + self.last - 1
        total = self.share(way * rel, yh)
        longest = self.half if (yh == 0) == (way > 0) else self.half - 1
        if rel < longest:
            before = base + 2 * rel + yh if rel + 1 < self.half else base + self.last - 1
            self.w.landed(self.into.at[before], self.ring + before, p.along_z(-way))
            total = total + self.into[before].astype(F32)
        self.out[slot] = total.astype(BF16)
        self.w.start(
            self.out.at[slot],
            self.into.at[slot],
            self.ring + slot,
            p.along_z(way),
            lambda: self.out.at[0],
        )

    def tick(self, step):
        if step == 0:
            self.pass_on(1, self.half, 0)
            self.pass_on(-1, self.half, 1)
            self.pass_on(1, self.half - 1, 1)
            self.pass_on(-1, self.half - 1, 0)
        else:
            rel = self.half - (step + 1) // 2
            first = step % 2
            if not first:
                rel -= 1
            if rel < 1:
                return
            self.pass_on(1, rel, 0 if first else 1)
            self.pass_on(-1, rel, 1 if first else 0)

    def spread(self):
        p = self.p
        for yh in range(2):
            total = self.share(0, yh)
            for way in (1, -1):
                slot = yh if way > 0 else self.last + yh
                self.w.landed(self.into.at[slot], self.ring + slot, p.along_z(-way))
                total = total + self.into[slot].astype(F32)
            for sub in range(p.lats):
                self.stage[yh, sub] = total[sub * self.lines : (sub + 1) * self.lines]
        for by in range(1, 2 * p.lats):
            yh, lat = p.in_plane(by)
            self.w.start(
                self.stage.at[yh, lat],
                self.land.at[by - 1],
                self.plane + by - 1,
                p.plane_device(by),
                lambda: self.land.at[0],
            )

    def collect(self):
        p = self.p
        total = self.stage[p.yh, p.lat]
        for by in range(1, 2 * p.lats):
            self.w.landed(
                self.land.at[by - 1], self.plane + by - 1, p.plane_device(2 * p.lats - by)
            )
            total = total + self.land[by - 1]
        self.full[p.lat] = total
        block = self.full.at[p.lat]
        for by in range(1, p.lats):
            self.w.start(
                block, block, self.along + by - 1, p.moved(by, 0), lambda: self.full.at[0]
            )

    def end(self):
        p = self.p
        for by in range(1, p.lats):
            lat = (p.lat - by + p.lats) % p.lats
            self.w.landed(self.full.at[lat], self.along + by - 1, (lat, p.lon))

    def write(self, store):
        for sub in range(self.p.lats):
            store(slice(sub * self.lines, (sub + 1) * self.lines), self.full[sub])


def shifted_blocks():
    for window in range(4):
        for quarter in range(4):
            i = 2 * (window // 2) + quarter // 2
            j = 2 * (window % 2) + quarter % 2
            yield i, j, window, quarter, i == 3, j == 3


def kernel(
    lats,
    lons,
    field,
    shard_one,
    shard_two,
    shard_three,
    out_field,
    out_one,
    out_two,
    out_three,
    moved,
    back,
    x_ref,
    up_ref,
    low_up,
    hidden_one,
    packed,
    probs_ref,
    attended,
    middle,
    result,
    hidden_two,
    active,
    grad_raised,
    grad_attended,
    grad_low,
    grad_packed,
    gains,
    sums,
    one,
    two,
    three,
    *rest,
):
    scatter_refs, (send_sem, recv_sem) = rest[:-2], rest[-2:]
    p = Place(lats, lons)
    wires = Wires(send_sem, recv_sem)
    width = x_ref.shape[1]
    hid = shard_two.shape[1]
    chunk = hid // p.rings
    rows = width // lons
    tokens = 4 * TOK
    scale = (width // HEADS) ** -0.5
    per = GROUP * HEADS // width
    head = width // HEADS
    groups = width // GROUP

    mark = Marks()
    mark("barrier")
    barrier = pltpu.get_barrier_semaphore()
    friends = [p.plane_device(by) for by in range(1, 2 * lats)]
    friends += [p.sibling, p.along_z(1), p.along_z(-1)]
    friends += [p.moved(0, 1), p.moved(0, -1), p.moved(1, 1), p.moved(-1, -1)]
    for friend in friends:
        pl.semaphore_signal(barrier, inc=1, device_id=friend, device_id_type=MESH)
    pl.semaphore_wait(barrier, len(friends))

    def beyond(by_rows, by_columns, sign):
        return p.moved(sign * int(by_rows), sign * int(by_columns))

    mark("gather_one")
    halo = wires.take(14)
    edge = [item for item in shifted_blocks() if item[4] or item[5]]
    first_weight, second_weight, third_weight = [
        Gather(p, wires, shard, whole)
        for shard, whole in ((shard_one, one), (shard_two, two), (shard_three, three))
    ]

    def send_halo(kind):
        for number, (i, j, window, quarter, down, over) in enumerate(edge):
            wires.start(
                field.at[(i + 1) % 4, (j + 1) % 4, kind],
                moved.at[window, quarter, kind],
                halo + 7 * kind + number,
                beyond(down, over, -1),
                lambda: moved.at[0, 0, 0],
            )

    def assemble(kind, windows, target):
        numbers = {item[2:4]: number for number, item in enumerate(edge)}
        for i, j, window, quarter, down, over in shifted_blocks():
            if window not in windows:
                continue
            if down or over:
                wires.landed(
                    moved.at[window, quarter, kind],
                    halo + 7 * kind + numbers[(window, quarter)],
                    beyond(down, over, 1),
                )
                block = moved[window, quarter, kind]
            else:
                block = field[i + 1, j + 1, kind]
            target[pl.ds(TOK * window + QUAD * quarter, PADQ)] = block.astype(F32)

    first_weight.tick(0)
    send_halo(0)
    first_weight.tick(1)
    assemble(0, (0,), x_ref)
    first_weight.tick(2)
    first_weight.tick(3)
    assemble(0, (1, 2), x_ref)
    first_weight.tick(4)
    first_weight.tick(5)
    assemble(0, (3,), x_ref)
    for step in range(6, first_weight.last + 1):
        first_weight.tick(step)
    second_weight.tick(0)
    send_halo(1)
    second_weight.tick(1)
    mark("gather_one_end")
    first_weight.end()

    def weight(ref, first, count):
        return ref[:, :, :, :, pl.ds(first, count)].reshape(width, count)

    mark("norm_one")
    turned = jnp.transpose(weight(one, 4 * width, 128).astype(F32), (1, 0))
    gains[0:8] = jnp.broadcast_to(turned[0:1], (8, width))
    gains[8:16] = jnp.broadcast_to(turned[64:65], (8, width))

    def by_rows(body):
        def run(window, _):
            body(pl.ds(pl.multiple_of(window * TOK, 16), TOK))
            return 0

        lax.fori_loop(0, 4, run, 0)

    def first_norm(at):
        normed, _ = layer_norm(x_ref[at])
        hidden_one[at] = (normed * gains[0:1]).astype(BF16)

    by_rows(first_norm)

    def columns(count, body):
        def run(number, _):
            body(pl.multiple_of(number * GROUP, GROUP), number)
            return 0

        lax.fori_loop(0, count, run, 0)

    def pack(first, number):
        packed[:, pl.ds(first, GROUP)] = nn(hidden_one[...], weight(one, first, GROUP)).astype(
            BF16
        )

    mark("qkv")
    columns(3 * groups, pack)

    mark("attend")
    lanes = lax.broadcasted_iota(jnp.int32, (TOK, GROUP), 1) // head
    late = lax.broadcasted_iota(jnp.int32, (TOK, TOK), 0) >= TOK // 2
    late_query = lax.broadcasted_iota(jnp.int32, (TOK, TOK), 1) >= TOK // 2
    differ = late != late_query

    def head_lanes(first):
        return pl.ds(pl.multiple_of(first, GROUP), GROUP)

    def at_turn(number, turns, turn_of):
        for turn in range(turn_of, len(turns), 2):
            if turns[turn]:

                def act(turn=turn):
                    for action in turns[turn]:
                        action()

                pl.when(number == turn // 2)(act)

    turns = [[] for _ in range(8 * groups)]
    for step in range(2, second_weight.last + 1):
        turns[2 * step - 3].append(functools.partial(second_weight.tick, step))
    turns[11].append(functools.partial(third_weight.tick, 0))
    turns[13].append(functools.partial(third_weight.tick, 1))
    turns[15].append(functools.partial(third_weight.tick, 2))

    def attend(number, _):
        window, group = number // groups, number % groups
        at = pl.ds(pl.multiple_of(window * TOK, 16), TOK)
        query = packed[at, head_lanes(group * GROUP)]
        keyed = packed[at, head_lanes(width + group * GROUP)]
        valued = packed[at, head_lanes(2 * width + group * GROUP)]
        split = jnp.logical_and(p.lat == lats - 1, window >= 2)
        bias = jnp.where(jnp.logical_and(differ, split), NEG, 0.0)
        value_turned = jnp.transpose(valued.astype(F32), (1, 0)).astype(BF16)
        parts = []
        for h in range(per):
            if h == per // 2:
                at_turn(number, turns, 0)
            mine = jnp.where(lanes == h, keyed, jnp.zeros_like(keyed))
            scores = nt(mine, query) * scale + bias
            raised = jnp.exp(scores - jnp.max(scores, axis=0, keepdims=True))
            probs = raised * (1.0 / jnp.sum(raised, axis=0, keepdims=True))
            probs_ref[number * per + h] = probs
            parts.append(nn(value_turned[h * head : (h + 1) * head], probs.astype(BF16)))
        attended[at, head_lanes(group * GROUP)] = jnp.transpose(
            jnp.concatenate(parts, axis=0), (1, 0)
        ).astype(BF16)
        at_turn(number, turns, 1)
        return 0

    lax.fori_loop(0, 4 * groups, attend, 0)
    mark("project")
    third_weight.tick(3)

    def project(first, number):
        middle[:, pl.ds(first, GROUP)] = x_ref[0:tokens, pl.ds(first, GROUP)] + nn(
            attended[...], weight(one, pl.multiple_of(3 * width + first, GROUP), GROUP)
        )

    columns(groups, project)
    third_weight.tick(4)
    assemble(1, (0, 1, 2, 3), up_ref)
    third_weight.tick(5)

    def second_norm(at):
        normed, _ = layer_norm(middle[at])
        hidden_two[at] = (normed * gains[8:9]).astype(BF16)
        low_up[at] = up_ref[at].astype(BF16)

    by_rows(second_norm)
    mark("gather_end")
    for step in range(6, third_weight.last + 1):
        third_weight.tick(step)
    second_weight.end()
    third_weight.end()

    scatter_down = Scatter(p, wires, scatter_refs[0:8], p.rings)
    scatter_up = Scatter(p, wires, scatter_refs[8:16], p.rings + 1)
    scatter_packed = [
        Scatter(p, wires, scatter_refs[16 + 8 * k : 24 + 8 * k], 1) for k in range(groups)
    ]
    every = slice(None)

    def across(first, count):
        return (every, every, every, pl.ds(first, count))

    def ring_place(rel):
        return (p.z + rel + p.rings) % p.rings

    def down_tick(step):
        if step % 2 == 0:
            needed = (p.rings // 2,) if step == 0 else ()
            near = p.rings // 2 - 1 - step // 2
            for rel in needed + (near, -near):
                place = ring_place(rel)
                scatter_down.traded((place,), place)
        scatter_down.tick(step)

    steps = p.rings - 2
    turns_feed = ((max(2, p.rings // 2 - 1), 0), (p.rings - 2, 1), (p.rings - 1, 2))

    def feed(number, _):
        rel = jnp.where(
            number % 2 == 1, p.rings // 2 - (number + 1) // 2, p.rings // 2 + number // 2
        )
        place = ring_place(rel)
        first = pl.ds(pl.multiple_of(place * chunk, 128), chunk)
        up_weight = two[:, :, :, :, first].reshape(width, chunk)
        raised_up = nn(hidden_two[...], up_weight)
        share = 0.5 * (1.0 + lax.erf(raised_up * 0.7071067811865476))
        act = (raised_up * share).astype(BF16)
        active[:, first] = act
        slope = share + raised_up * jnp.exp(-0.5 * raised_up * raised_up) * 0.3989422804014327
        grad_down = tn(act, low_up[...])
        scatter_down.put((place,), grad_down.reshape(2, 2, chunk // 4, width))
        scatter_down.trade((place,), place)
        down_weight = three[place].reshape(chunk, width)
        grads = (nt(low_up[...], down_weight) * slope).astype(BF16)
        grad_raised[:, first] = grads
        grad_up = tn(hidden_two[...], grads)
        where = across(pl.multiple_of(place * chunk, 128), chunk)
        scatter_up.put(where, grad_up.reshape(p.rings, 2, 2, rows, chunk))
        scatter_up.trade(where, place)
        for turn, step in turns_feed:
            if step < steps:
                pl.when(number == turn)(functools.partial(down_tick, step))
        return 0

    mark("feed")
    lax.fori_loop(0, p.rings, feed, 0)

    def lower(first, number):
        down = three[:, :, :, :, pl.ds(first, GROUP)].reshape(hid, GROUP)
        result[0:tokens, pl.ds(first, GROUP)] = middle[:, pl.ds(first, GROUP)] + nn(
            active[...], down
        )

    mark("lower")
    columns(groups, lower)
    for step in range(3, min(steps, 4)):
        down_tick(step)

    returns = wires.take(14)

    def send_back(source, kind):
        number = 0
        for i, j, window, quarter, down, over in shifted_blocks():
            first = TOK * window + QUAD * quarter
            block = source[pl.ds(first, PADQ)].astype(BF16)
            target = out_field.at[(i + 1) % 4, (j + 1) % 4, kind]
            if down or over:
                place = back.at[number, kind]
                place[...] = block
                index = returns + 7 * kind + number
                wires.start(place, target, index, beyond(down, over, 1), lambda: back.at[0, 0])
                number += 1
            else:
                target[...] = block

    mark("return_out")
    send_back(result, 0)
    for step in range(4, min(steps, 5)):
        down_tick(step)

    def raise_back(first, number):
        share = p.rings // groups
        up_rows = two[pl.ds(number * share, share)].reshape(GROUP, hid)
        result[0:tokens, pl.ds(first, GROUP)] = nt(grad_raised[...], up_rows)

    mark("raise_back")
    columns(groups, raise_back)
    for step in range(5, steps):
        down_tick(step)

    sums[...] = jnp.zeros_like(sums)

    def second_back(at):
        normed, inverse = layer_norm(middle[at])
        through, total = norm_back(result[at], normed, inverse, gains[8:9])
        sums[8:16] += jnp.broadcast_to(total, (8, width))
        grad_middle = up_ref[at] + through
        up_ref[at] = grad_middle
        grad_low[at] = grad_middle.astype(BF16)

    mark("norm_two_back")
    by_rows(second_back)

    def split_columns(value):
        return value.reshape(p.rings, 2, 2, rows, value.shape[1])

    def project_back(first, number):
        grad = tn(attended[...], grad_low[:, pl.ds(first, GROUP)])
        scatter_up.put(across(pl.multiple_of(hid + first, GROUP), GROUP), split_columns(grad))
        share = p.rings // groups
        proj_rows = one[pl.ds(number * share, share), :, :, :, pl.ds(3 * width, width)]
        grad_attended[:, pl.ds(first, GROUP)] = nt(
            grad_low[...], proj_rows.reshape(GROUP, width)
        ).astype(BF16)

    mark("project_back")
    columns(groups, project_back)
    scatter_up.trade(across(hid, width), p.rings)
    mark("spread_down")
    scatter_down.traded((ring_place(0),), ring_place(0))
    scatter_down.spread()

    def trade_up(number, _):
        where = across(pl.multiple_of(number * chunk, 128), chunk)
        scatter_up.traded(where, number)
        return 0

    lax.fori_loop(0, p.rings, trade_up, 0)
    scatter_up.traded(across(hid, width), p.rings)
    scatter_up.tick(0)

    def attend_back(group, turns, number, _):
        window = number
        at = pl.ds(pl.multiple_of(window * TOK, 16), TOK)
        query = packed[at, head_lanes(group * GROUP)]
        keyed = packed[at, head_lanes(width + group * GROUP)]
        valued = packed[at, head_lanes(2 * width + group * GROUP)]
        upstream = grad_attended[at, head_lanes(group * GROUP)]
        key_turned = jnp.transpose(keyed.astype(F32), (1, 0)).astype(BF16)
        grad_key = jnp.zeros((TOK, GROUP), F32)
        grad_value = jnp.zeros((TOK, GROUP), F32)
        parts = []
        for h in range(per):
            if h == per // 2:
                at_turn(number, turns, 0)
            probs = probs_ref[(number * groups + group) * per + h]
            mine = lanes == h
            grad_probs = nt(jnp.where(mine, valued, jnp.zeros_like(valued)), upstream)
            grad_value = jnp.where(mine, nn(probs.astype(BF16), upstream), grad_value)
            inner = jnp.sum(grad_probs * probs, axis=0, keepdims=True)
            grad_scores = (probs * (grad_probs - inner) * scale).astype(BF16)
            grad_key = jnp.where(mine, nn(grad_scores, query), grad_key)
            parts.append(nn(key_turned[h * head : (h + 1) * head], grad_scores))
        grad_query = jnp.transpose(jnp.concatenate(parts, axis=0), (1, 0))
        grad_packed[at, head_lanes(group * GROUP)] = grad_query.astype(BF16)
        grad_packed[at, head_lanes(width + group * GROUP)] = grad_key.astype(BF16)
        grad_packed[at, head_lanes(2 * width + group * GROUP)] = grad_value.astype(BF16)
        at_turn(number, turns, 1)
        return 0

    def pack_back(group):
        def run(part, _):
            first = pl.multiple_of(part * width + group * GROUP, GROUP)
            grad = tn(hidden_one[...], grad_packed[:, pl.ds(first, GROUP)])
            where = across(pl.multiple_of(part * GROUP, GROUP), GROUP)
            scatter_packed[group].put(where, split_columns(grad))
            return 0

        lax.fori_loop(0, 3, run, 0)

    turns_one = [[] for _ in range(8)]
    turns_one[1].append(scatter_down.collect)
    for step in range(1, steps):
        turns_one[step + 1].append(functools.partial(scatter_up.tick, step))
    turns_one[7].append(scatter_down.end)
    turns_two = [[] for _ in range(8)]
    turns_two[0].append(scatter_up.spread)
    for step in range(1, steps):
        turns_two[step + 1].append(functools.partial(scatter_packed[0].tick, step))
    turns_two[3].append(scatter_up.collect)
    turns_two[7].append(scatter_up.end)

    mark("attend_back")
    lax.fori_loop(0, 4, functools.partial(attend_back, 0, turns_one), 0)
    mark("pack_back")
    pack_back(0)
    full = (every, every, every, every)
    scatter_packed[0].trade(full, 0)
    scatter_packed[0].traded(full, 0)
    scatter_packed[0].tick(0)
    mark("attend_back_two")
    lax.fori_loop(0, 4, functools.partial(attend_back, 1, turns_two), 0)
    mark("pack_back_two")
    scatter_packed[0].spread()

    def unpack(first, number):
        share = p.rings // groups
        rows_here = one[pl.ds(number * share, share), :, :, :, pl.ds(0, 3 * width)]
        result[0:tokens, pl.ds(first, GROUP)] = nt(
            grad_packed[...], rows_here.reshape(GROUP, 3 * width)
        )

    columns(groups, unpack)

    def first_back(at):
        normed, inverse = layer_norm(x_ref[at])
        through, total = norm_back(result[at], normed, inverse, gains[0:1])
        sums[0:8] += jnp.broadcast_to(total, (8, width))
        up_ref[at] = up_ref[at] + through

    mark("norm_one_back")
    by_rows(first_back)
    pack_back(1)
    line = lax.broadcasted_iota(jnp.int32, (128, width), 0)
    both = jnp.where(line < 64, sums[0:1], sums[8:9])
    last = scatter_packed[1]
    last.put(across(3 * GROUP, 128), split_columns(jnp.transpose(both, (1, 0))))
    mark("trade_last")
    last.trade(full, 0)
    scatter_packed[0].collect()
    send_back(up_ref, 1)
    last.traded(full, 0)
    mark("ring_last")
    for step in range(steps):
        last.tick(step)
    mark("plane_last")
    last.spread()

    scatter_packed[0].end()

    def store_down(at, value):
        out_three[at] = value

    def store_up(at, value):
        out_two[at] = value

    def store_packed(group, at, value):
        for part in range(3):
            out_one[at, part * width + group * GROUP : part * width + (group + 1) * GROUP] = value[
                :, part * GROUP : (part + 1) * GROUP
            ]
        if group == 1:
            out_one[at, 3 * width :] = value[:, 3 * GROUP :]

    scatter_down.write(store_down)
    scatter_up.write(store_up)
    scatter_packed[0].write(functools.partial(store_packed, 0))
    mark("collect_last")
    last.collect()
    number = 0
    for i, j, window, quarter, down, over in shifted_blocks():
        if down or over:
            for kind in range(2):
                wires.landed(
                    out_field.at[(i + 1) % 4, (j + 1) % 4, kind],
                    returns + 7 * kind + number,
                    beyond(down, over, -1),
                )
            number += 1
    last.end()
    last.write(functools.partial(store_packed, 1))
    mark("finish")
    wires.finish(p.sibling)
    mark()


def blocks_of(field):
    height, breadth, depth = field.shape
    shaped = field.reshape(height // SHIFT, SHIFT, breadth // SHIFT, SHIFT, depth)
    shaped = shaped.transpose(0, 2, 1, 3, 4).reshape(4, 4, QUAD, depth)
    return jnp.pad(shaped, ((0, 0), (0, 0), (0, PADQ - QUAD), (0, 0)))


def field_of(blocks):
    depth = blocks.shape[-1]
    shaped = blocks[:, :, :QUAD].reshape(4, 4, SHIFT, SHIFT, depth)
    return shaped.transpose(0, 2, 1, 3, 4).reshape(4 * SHIFT, 4 * SHIFT, depth)


def body(
    lats,
    lons,
    cells,
    cotangent,
    land,
    land_embed,
    qkv_weight,
    proj_weight,
    up_weight,
    down_weight,
    gain_one,
    gain_two,
):
    start = (
        cells.astype(F32) + land[:, :, None].astype(F32) * land_embed[None, None, :]
    ).astype(BF16)
    field = jnp.stack([blocks_of(start), blocks_of(cotangent)], axis=2)
    rows, hid = up_weight.shape
    width = cells.shape[2]
    deep = down_weight.shape[0]
    tokens = 4 * TOK
    rings = lons // 4
    shard_one = jnp.concatenate(
        [
            qkv_weight,
            proj_weight,
            jnp.broadcast_to(gain_one[:, None], (rows, 64)),
            jnp.broadcast_to(gain_two[:, None], (rows, 64)),
        ],
        axis=1,
    )

    def scatter_scratch(lines, across):
        return [
            pltpu.VMEM((rings, 2, lines, across), F32),
            pltpu.VMEM((rings, 2, lines, across), BF16),
            pltpu.VMEM((rings, 2, lines, across), BF16),
            pltpu.VMEM((2 * rings - 2, lines, across), BF16),
            pltpu.VMEM((2 * rings - 2, lines, across), BF16),
            pltpu.VMEM((2, lats, lines // lats, across), F32),
            pltpu.VMEM((2 * lats - 1, lines // lats, across), F32),
            pltpu.VMEM((lats, lines // lats, across), F32),
        ]

    scratch = [
        pltpu.VMEM((4, 4, 2, PADQ, width), BF16),
        pltpu.VMEM((7, 2, PADQ, width), BF16),
        pltpu.VMEM((tokens + 16, width), F32),
        pltpu.VMEM((tokens + 16, width), F32),
        pltpu.VMEM((tokens, width), BF16),
        pltpu.VMEM((tokens, width), BF16),
        pltpu.VMEM((tokens, 3 * width), BF16),
        pltpu.VMEM((4 * HEADS, TOK, TOK), F32),
        pltpu.VMEM((tokens, width), BF16),
        pltpu.VMEM((tokens, width), F32),
        pltpu.VMEM((tokens + 16, width), F32),
        pltpu.VMEM((tokens, width), BF16),
        pltpu.VMEM((tokens, hid), BF16),
        pltpu.VMEM((tokens, hid), BF16),
        pltpu.VMEM((tokens, width), BF16),
        pltpu.VMEM((tokens, width), BF16),
        pltpu.VMEM((tokens, 3 * width), BF16),
        pltpu.VMEM((16, width), F32),
        pltpu.VMEM((16, width), F32),
        pltpu.VMEM((rings, 2, 2, rows, 4 * width + 128), BF16),
        pltpu.VMEM((rings, 2, 2, rows, hid), BF16),
        pltpu.VMEM((rings, 2, 2, deep, width), BF16),
    ]
    scratch += scatter_scratch(deep, width)
    scratch += scatter_scratch(rows, hid + width)
    scratch += scatter_scratch(rows, 3 * GROUP)
    scratch += scatter_scratch(rows, 3 * GROUP + 128)
    wires = 14 + 14 + 3 * (3 * rings - 1)
    wires += 4 * (2 * rings - 2 + 3 * lats - 2) + 2 * rings + 3
    scratch += [pltpu.SemaphoreType.DMA((wires,)), pltpu.SemaphoreType.DMA((wires,))]
    vmem = pl.BlockSpec(memory_space=pltpu.VMEM)
    out_field, one, two, three = pl.pallas_call(
        functools.partial(kernel, lats, lons),
        out_shape=(
            jax.ShapeDtypeStruct((4, 4, 2, PADQ, width), BF16),
            jax.ShapeDtypeStruct((rows, 3 * width + 128), F32),
            jax.ShapeDtypeStruct((rows, hid + width), F32),
            jax.ShapeDtypeStruct((deep, width), F32),
        ),
        in_specs=[vmem] * 4,
        out_specs=(vmem,) * 4,
        scratch_shapes=scratch,
        compiler_params=pltpu.CompilerParams(
            collective_id=0, has_side_effects=True, vmem_limit_bytes=63 * 2**20
        ),
        name="block",
    )(field, shard_one, up_weight, down_weight)
    return (
        field_of(out_field[:, :, 0]),
        field_of(out_field[:, :, 1]),
        one[:, : 3 * width],
        two[:, hid:],
        two[:, :hid],
        three,
        one[:, 3 * width],
        one[:, 3 * width + 64],
    )


def solution(mesh):
    placed = (
        P("lat", "lon", None),
        P("lat", "lon", None),
        P("lat", "lon"),
        P(),
        P("lon", None),
        P("lon", None),
        P("lon", None),
        P("lon", None),
        P("lon"),
        P("lon"),
    )
    return jax.shard_map(
        functools.partial(body, mesh.shape["lat"], mesh.shape["lon"]),
        mesh=mesh,
        in_specs=placed,
        out_specs=(
            P("lat", "lon", None),
            P("lat", "lon", None),
            P("lon", None),
            P("lon", None),
            P("lon", None),
            P("lon", None),
            P("lon"),
            P("lon"),
        ),
        check_vma=False,
    )
```

```python
import functools

import jax
import jax.numpy as jnp
from jax import lax
from jax.experimental import pallas as pl
from jax.experimental.pallas import tpu as pltpu
from jax.sharding import PartitionSpec as P

HEADS = 16
WIN = 12
SHIFT = 6
EPS = 1e-5
NEG = -1e30
TOK = WIN * WIN
QUAD = SHIFT * SHIFT
PADQ = 48
GROUP = 256
F32 = jnp.float32
BF16 = jnp.bfloat16
MESH = pl.DeviceIdType.MESH


def nn(a, b):
    return lax.dot_general(a, b, (((1,), (0,)), ((), ())), preferred_element_type=F32)


def nt(a, b):
    return lax.dot_general(a, b, (((1,), (1,)), ((), ())), preferred_element_type=F32)


def tn(a, b):
    return lax.dot_general(a, b, (((0,), (0,)), ((), ())), preferred_element_type=F32)


def layer_norm(x):
    centred = x - jnp.mean(x, axis=-1, keepdims=True)
    spread = jnp.mean(centred * centred, axis=-1, keepdims=True)
    inverse = lax.rsqrt(spread + EPS)
    return centred * inverse, inverse


def norm_back(upstream, normed, inverse, gain):
    scaled = upstream * gain
    inner = (
        scaled
        - jnp.mean(scaled, axis=-1, keepdims=True)
        - normed * jnp.mean(scaled * normed, axis=-1, keepdims=True)
    )
    return inner * inverse, jnp.sum(upstream * normed, axis=0, keepdims=True)


class Marks:
    def __init__(self):
        self.open = None

    def __call__(self, name=None):
        if self.open is not None:
            self.open.__exit__(None, None, None)
        self.open = None
        if name is not None:
            self.open = jax.named_scope(name)
            self.open.__enter__()


class Place:
    def __init__(self, lats, lons):
        self.lats, self.lons, self.rings = lats, lons, lons // 4
        self.lat = lax.axis_index("lat")
        self.lon = lax.axis_index("lon")
        self.z = self.lon // 4
        self.yh = (self.lon // 2) % 2
        self.core = self.lon % 2
        self.sibling = (self.lat, self.lon + 1 - 2 * self.core)
        near = self.lat + 1 - 2 * (self.lat % 2)
        self.partner = (near, self.z * 4 + (1 - self.yh) * 2 + self.core)

    def along_z(self, by):
        z = (self.z + by + self.rings) % self.rings
        return (self.lat, z * 4 + self.yh * 2 + self.core)

    def moved(self, by_lat, by_lon):
        lat = (self.lat + by_lat + self.lats) % self.lats
        lon = (self.lon + by_lon + self.lons) % self.lons
        return (lat, lon)

    def along_y(self, by):
        y = (self.yh * 2 + self.lat % 2 + by) % 4
        return (self.lat // 2 * 2 + y % 2, self.z * 4 + (y // 2) * 2 + self.core)


class Wires:
    def __init__(self, send, recv):
        self.send, self.recv, self.used, self.sent = send, recv, 0, []

    def take(self, count):
        first = self.used
        self.used += count
        return first

    def copy(self, src, dst, index, device):
        return pltpu.make_async_remote_copy(
            src_ref=src,
            dst_ref=dst,
            send_sem=self.send.at[index],
            recv_sem=self.recv.at[index],
            device_id=device,
            device_id_type=MESH,
        )

    def start(self, src, dst, index, device, until=None):
        self.copy(src, dst, index, device).start()
        if until is not None:
            self.sent.append((until, index))

    def landed(self, ref, index, device):
        self.copy(ref, ref, index, device).wait_recv()

    def finish(self, device):
        for view, index in self.sent:
            ref = view()
            self.copy(ref, ref, index, device).wait_send()


class Gather:
    def __init__(self, place, wires, shard, whole):
        self.p, self.w, self.shard, self.whole = place, wires, shard, whole
        self.half = place.rings // 2
        self.last = 2 * self.half
        self.far = wires.take(1)
        self.way = {1: wires.take(self.last - 1), -1: wires.take(self.last - 1)}
        self.side = wires.take(place.rings)

    def slot(self, rel, other):
        p = self.p
        yh = 1 - p.yh if other else p.yh
        return self.whole.at[(p.z - rel + p.rings) % p.rings, yh, p.core]

    def pair(self, rel, core):
        p = self.p
        return self.whole.at[(p.z - rel + p.rings) % p.rings, :, core]

    def forward(self, way, hop, other):
        if hop == self.half - 1 and other != (way < 0):
            return
        index = self.way[way] + (2 * hop + other if hop < self.half - 1 else 2 * hop)
        block = self.slot(way * hop, other)
        self.w.start(block, block, index, self.p.along_z(way), lambda: self.whole.at[0, 0, 0])

    def landed(self, way, hop, other):
        index = self.way[way] + (2 * (hop - 1) + other if hop < self.half else 2 * (hop - 1))
        self.w.landed(self.slot(way * hop, other), index, self.p.along_z(-way))

    def share(self, rel):
        p = self.p
        index = self.side + rel % p.rings
        block = self.pair(rel, p.core)
        self.w.start(block, block, index, p.sibling, lambda: self.whole.at[0, :, 0])

    def tick(self, step):
        p = self.p
        if step == 0:
            here = self.slot(0, 0)
            here[...] = self.shard[...]
            for way in (1, -1):
                self.forward(way, 0, 0)
            self.w.start(self.shard, here, self.far, p.partner, lambda: self.shard)
        elif step == 1:
            self.w.landed(self.slot(0, 1), self.far, p.partner)
            for way in (1, -1):
                self.forward(way, 0, 1)
            self.share(0)
        elif step < self.last:
            hop, other = step // 2, step % 2
            for way in (1, -1):
                self.landed(way, hop, other)
                self.forward(way, hop, other)
            if other:
                for way in (1, -1):
                    self.share(way * hop)
        else:
            self.landed(1, self.half, 0)
            self.landed(-1, self.half, 1)
            self.share(self.half)

    def end(self):
        p = self.p
        for rel in range(p.rings):
            self.w.landed(self.pair(rel, 1 - p.core), self.side + rel, p.sibling)


class Scatter:
    def __init__(self, place, wires, refs, pieces, axis):
        self.p, self.w, self.pieces, self.axis = place, wires, pieces, axis
        self.own, self.away, self.near, self.give, self.got, self.sum = refs[:6]
        self.out, self.into, self.stage, self.land, self.full = refs[6:]
        self.size = {"x": place.lats // 2, "y": 4}
        self.other = "y" if axis == "x" else "x"
        self.count = self.sum.shape[3]
        self.exchange = wires.take(pieces)
        self.over = wires.take(3)
        self.ring = wires.take(place.rings - 1)
        self.plane = wires.take(3)
        self.along = wires.take(3)
        self.x, self.y = place.lat // 2, place.yh * 2 + place.lat % 2

    def put(self, where, value):
        first, second = value[..., 0, :, :], value[..., 1, :, :]
        mine = self.p.core == 0
        self.own[where] = jnp.where(mine, first, second)
        self.away[where] = jnp.where(mine, second, first).astype(BF16)

    def trade(self, where, index):
        self.w.copy(
            self.away.at[where], self.near.at[where], self.exchange + index, self.p.sibling
        ).start()

    def traded(self, where, index):
        copy = self.w.copy(
            self.away.at[where], self.near.at[where], self.exchange + index, self.p.sibling
        )
        copy.wait_send()
        copy.wait_recv()

    def at(self, axis, by):
        p = self.p
        size = self.size[axis]
        if axis == "x":
            x = (self.x + by + size) % size
            return x, (x * 2 + p.lat % 2, p.lon)
        y = (self.y + by + size) % size
        return y, (self.x * 2 + y % 2, p.z * 4 + (y // 2) * 2 + p.core)

    def quarter(self, number):
        every = slice(None)
        first = pl.multiple_of(number * self.count, 128)
        at = (every, every, every, pl.ds(first, self.count))
        return self.own[at] + self.near[at].astype(F32)

    def cross(self):
        for by in range(1, self.size[self.axis]):
            number, device = self.at(self.axis, by)
            self.give[by - 1] = self.quarter(number).astype(BF16)
            source = self.give.at[by - 1]
            self.w.start(
                source, self.got.at[by - 1], self.over + by - 1, device, lambda: self.give.at[0]
            )

    def crossed(self):
        p = self.p
        total = self.quarter(self.at(self.axis, 0)[0])
        for by in range(1, self.size[self.axis]):
            device = self.at(self.axis, -by)[1]
            self.w.landed(self.got.at[by - 1], self.over + by - 1, device)
            total = total + self.got[by - 1].astype(F32)
        self.sum[...] = total
        for by in range(1, p.rings):
            self.out[by - 1] = self.sum[(p.z + by) % p.rings].astype(BF16)
            source = self.out.at[by - 1]
            self.w.start(
                source,
                self.into.at[by - 1],
                self.ring + by - 1,
                p.along_z(by),
                lambda: self.out.at[0],
            )

    def spread(self):
        p = self.p
        total = self.sum[p.z]
        for by in range(1, p.rings):
            self.w.landed(self.into.at[by - 1], self.ring + by - 1, p.along_z(-by))
            total = total + self.into[by - 1].astype(F32)
        self.stage[...] = total
        here = self.at(self.other, 0)[0]
        self.land[here] = self.stage[...]
        for by in range(1, self.size[self.other]):
            device = self.at(self.other, by)[1]
            self.w.start(
                self.stage,
                self.land.at[here],
                self.plane + by - 1,
                device,
                lambda: self.land.at[0],
            )

    def collect(self):
        p = self.p
        size = self.size[self.other]
        for by in range(1, size):
            number, device = self.at(self.other, -by)
            self.w.landed(self.land.at[number], self.plane + by - 1, device)
        total = self.land[0]
        for number in range(1, size):
            total = total + self.land[number]
        mine = self.at(self.other, 0)[0]
        self.land[mine] = total
        here = self.at(self.axis, 0)[0]
        self.full[here] = self.land[mine, p.yh]
        for by in range(1, self.size[self.axis]):
            number, device = self.at(self.axis, by)
            yh = p.yh if self.axis == "x" else number // 2
            self.w.start(
                self.land.at[mine, yh],
                self.full.at[here],
                self.along + by - 1,
                device,
                lambda: self.full.at[0],
            )

    def end(self):
        for by in range(1, self.size[self.axis]):
            number, device = self.at(self.axis, -by)
            self.w.landed(self.full.at[number], self.along + by - 1, device)

    def columns(self):
        return jnp.concatenate(
            [self.full[number] for number in range(self.size[self.axis])], axis=1
        )


def shifted_blocks():
    for window in range(4):
        for quarter in range(4):
            i = 2 * (window // 2) + quarter // 2
            j = 2 * (window % 2) + quarter % 2
            yield i, j, window, quarter, i == 3, j == 3


def kernel(
    lats,
    lons,
    field,
    shard_one,
    shard_two,
    shard_three,
    out_field,
    out_one,
    out_two,
    out_three,
    moved,
    back,
    x_ref,
    up_ref,
    low_up,
    hidden_one,
    packed,
    probs_ref,
    attended,
    middle,
    result,
    hidden_two,
    active,
    grad_raised,
    grad_attended,
    grad_low,
    grad_packed,
    gains,
    sums,
    one,
    two,
    three,
    *rest,
):
    scatter_refs, (send_sem, recv_sem) = rest[:-2], rest[-2:]
    p = Place(lats, lons)
    wires = Wires(send_sem, recv_sem)
    width = x_ref.shape[1]
    hid = shard_two.shape[1]
    chunk = hid // p.rings
    rows = width // lons
    tokens = 4 * TOK
    scale = (width // HEADS) ** -0.5
    per = GROUP * HEADS // width
    head = width // HEADS
    groups = width // GROUP

    mark = Marks()
    mark("barrier")
    barrier = pltpu.get_barrier_semaphore()
    friends = [p.sibling] + [p.along_z(by) for by in range(1, p.rings)]
    friends += [p.moved(2 * by, 0) for by in range(1, lats // 2)]
    friends += [p.along_y(by) for by in range(1, 4)]
    for by_lat, by_lon in ((1, 0), (0, 1), (1, 1)):
        friends += [p.moved(by_lat, by_lon), p.moved(-by_lat, -by_lon)]
    for friend in friends:
        pl.semaphore_signal(barrier, inc=1, device_id=friend, device_id_type=MESH)
    pl.semaphore_wait(barrier, len(friends))

    def beyond(by_rows, by_columns, sign):
        return p.moved(sign * int(by_rows), sign * int(by_columns))

    mark("gather_one")
    halo = wires.take(14)
    edge = [item for item in shifted_blocks() if item[4] or item[5]]
    first_weight, second_weight, third_weight = [
        Gather(p, wires, shard, whole)
        for shard, whole in ((shard_one, one), (shard_two, two), (shard_three, three))
    ]

    def send_halo(kind):
        for number, (i, j, window, quarter, down, over) in enumerate(edge):
            wires.start(
                field.at[(i + 1) % 4, (j + 1) % 4, kind],
                moved.at[window, quarter, kind],
                halo + 7 * kind + number,
                beyond(down, over, -1),
                lambda: moved.at[0, 0, 0],
            )

    def assemble(kind, windows, target):
        numbers = {item[2:4]: number for number, item in enumerate(edge)}
        for i, j, window, quarter, down, over in shifted_blocks():
            if window not in windows:
                continue
            if down or over:
                wires.landed(
                    moved.at[window, quarter, kind],
                    halo + 7 * kind + numbers[(window, quarter)],
                    beyond(down, over, 1),
                )
                block = moved[window, quarter, kind]
            else:
                block = field[i + 1, j + 1, kind]
            target[pl.ds(TOK * window + QUAD * quarter, PADQ)] = block.astype(F32)

    first_weight.tick(0)
    send_halo(0)
    for step in range(1, first_weight.last):
        first_weight.tick(step)
    second_weight.tick(0)
    third_weight.tick(0)
    first_weight.tick(first_weight.last)
    second_weight.tick(1)
    third_weight.tick(1)
    send_halo(1)
    mark("gather_one_end")
    first_weight.end()
    assemble(0, (0, 1, 2, 3), x_ref)

    def weight(ref, first, count):
        return ref[:, :, :, :, pl.ds(first, count)].reshape(width, count)

    mark("norm_one")
    turned = jnp.transpose(weight(one, 4 * width, 128).astype(F32), (1, 0))
    gains[0:8] = jnp.broadcast_to(turned[0:1], (8, width))
    gains[8:16] = jnp.broadcast_to(turned[64:65], (8, width))

    def by_rows(body):
        def run(window, _):
            body(pl.ds(pl.multiple_of(window * TOK, 16), TOK))
            return 0

        lax.fori_loop(0, 4, run, 0)

    def first_norm(at):
        normed, _ = layer_norm(x_ref[at])
        hidden_one[at] = (normed * gains[0:1]).astype(BF16)

    by_rows(first_norm)

    def columns(count, body):
        def run(number, _):
            body(pl.multiple_of(number * GROUP, GROUP), number)
            return 0

        lax.fori_loop(0, count, run, 0)

    def pack(first, number):
        packed[:, pl.ds(first, GROUP)] = nn(hidden_one[...], weight(one, first, GROUP)).astype(
            BF16
        )

    mark("qkv")
    columns(3 * groups, pack)

    mark("attend")
    lanes = lax.broadcasted_iota(jnp.int32, (TOK, GROUP), 1) // head
    late = lax.broadcasted_iota(jnp.int32, (TOK, TOK), 0) >= TOK // 2
    late_query = lax.broadcasted_iota(jnp.int32, (TOK, TOK), 1) >= TOK // 2
    differ = late != late_query

    def head_lanes(first):
        return pl.ds(pl.multiple_of(first, GROUP), GROUP)

    def at_turn(number, turns, turn_of):
        for turn in range(turn_of, len(turns), 2):
            if turns[turn]:

                def act(turn=turn):
                    for action in turns[turn]:
                        action()

                pl.when(number == turn // 2)(act)

    turns = [[] for _ in range(8 * groups)]
    for step in range(2, min(6, second_weight.last)):
        turns[4 * step - 7] += [
            functools.partial(second_weight.tick, step),
            functools.partial(third_weight.tick, step),
        ]

    def weights_tick(step):
        if step <= second_weight.last:
            second_weight.tick(step)
            third_weight.tick(step)

    def attend(number, _):
        window, group = number // groups, number % groups
        at = pl.ds(pl.multiple_of(window * TOK, 16), TOK)
        query = packed[at, head_lanes(group * GROUP)]
        keyed = packed[at, head_lanes(width + group * GROUP)]
        valued = packed[at, head_lanes(2 * width + group * GROUP)]
        split = jnp.logical_and(p.lat == lats - 1, window >= 2)
        bias = jnp.where(jnp.logical_and(differ, split), NEG, 0.0)
        value_turned = jnp.transpose(valued.astype(F32), (1, 0)).astype(BF16)
        parts = []
        for h in range(per):
            if h == per // 2:
                at_turn(number, turns, 0)
            mine = jnp.where(lanes == h, keyed, jnp.zeros_like(keyed))
            scores = nt(mine, query) * scale + bias
            raised = jnp.exp(scores - jnp.max(scores, axis=0, keepdims=True))
            probs = raised * (1.0 / jnp.sum(raised, axis=0, keepdims=True))
            probs_ref[number * per + h] = probs
            parts.append(nn(value_turned[h * head : (h + 1) * head], probs.astype(BF16)))
        attended[at, head_lanes(group * GROUP)] = jnp.transpose(
            jnp.concatenate(parts, axis=0), (1, 0)
        ).astype(BF16)
        at_turn(number, turns, 1)
        return 0

    lax.fori_loop(0, 4 * groups, attend, 0)
    mark("project")

    def project(first, number):
        middle[:, pl.ds(first, GROUP)] = x_ref[0:tokens, pl.ds(first, GROUP)] + nn(
            attended[...], weight(one, pl.multiple_of(3 * width + first, GROUP), GROUP)
        )

    columns(groups, project)
    weights_tick(6)
    assemble(1, (0, 1, 2, 3), up_ref)

    def second_norm(at):
        normed, _ = layer_norm(middle[at])
        hidden_two[at] = (normed * gains[8:9]).astype(BF16)
        low_up[at] = up_ref[at].astype(BF16)

    by_rows(second_norm)
    mark("gather_end")
    if second_weight.last < 6:
        weights_tick(second_weight.last)
    weights_tick(7)
    weights_tick(8)
    second_weight.end()
    third_weight.end()

    def scatter(number, pieces, axis):
        return Scatter(p, wires, scatter_refs[11 * number : 11 * number + 11], pieces, axis)

    scatter_down = scatter(0, p.rings, "y")
    scatter_up = scatter(1, p.rings + 1, "x")
    scatter_query = [scatter(2, 1, "y"), scatter(3, 1, "x")]
    scatter_value = [scatter(4, 1, "x"), scatter(5, 1, "y")]
    every = slice(None)

    def across(first, count):
        return (every, every, every, pl.ds(first, count))

    def ring_place(rel):
        return (p.z + rel + p.rings) % p.rings

    def feed(number, _):
        rel = jnp.where(
            number % 2 == 1, p.rings // 2 - (number + 1) // 2, p.rings // 2 + number // 2
        )
        place = ring_place(rel)
        first = pl.ds(pl.multiple_of(place * chunk, 128), chunk)
        up_weight = two[:, :, :, :, first].reshape(width, chunk)
        raised_up = nn(hidden_two[...], up_weight)
        share = 0.5 * (1.0 + lax.erf(raised_up * 0.7071067811865476))
        act = (raised_up * share).astype(BF16)
        active[:, first] = act
        slope = share + raised_up * jnp.exp(-0.5 * raised_up * raised_up) * 0.3989422804014327
        grad_down = tn(act, low_up[...])
        scatter_down.put((place,), grad_down.reshape(2, 2, chunk // 4, width))
        scatter_down.trade((place,), place)
        down_weight = three[place].reshape(chunk, width)
        grads = (nt(low_up[...], down_weight) * slope).astype(BF16)
        grad_raised[:, first] = grads
        grad_up = tn(hidden_two[...], grads)
        where = across(pl.multiple_of(place * chunk, 128), chunk)
        scatter_up.put(where, grad_up.reshape(p.rings, 2, 2, rows, chunk))
        scatter_up.trade(where, place)
        return 0

    mark("feed")
    lax.fori_loop(0, p.rings, feed, 0)

    def lower(first, number):
        down = three[:, :, :, :, pl.ds(first, GROUP)].reshape(hid, GROUP)
        result[0:tokens, pl.ds(first, GROUP)] = middle[:, pl.ds(first, GROUP)] + nn(
            active[...], down
        )

    def trade_all(number, _):
        scatter_down.traded((number,), number)
        scatter_up.traded(across(pl.multiple_of(number * chunk, 128), chunk), number)
        return 0

    mark("lower")
    columns(groups, lower)

    returns = wires.take(14)

    def send_back(source, kind):
        number = 0
        for i, j, window, quarter, down, over in shifted_blocks():
            first = TOK * window + QUAD * quarter
            block = source[pl.ds(first, PADQ)].astype(BF16)
            target = out_field.at[(i + 1) % 4, (j + 1) % 4, kind]
            if down or over:
                place = back.at[number, kind]
                place[...] = block
                index = returns + 7 * kind + number
                wires.start(place, target, index, beyond(down, over, 1), lambda: back.at[0, 0])
                number += 1
            else:
                target[...] = block

    mark("return_out")
    send_back(result, 0)
    lax.fori_loop(0, p.rings, trade_all, 0)
    scatter_down.cross()

    def raise_back(first, number):
        share = p.rings // groups
        up_rows = two[pl.ds(number * share, share)].reshape(GROUP, hid)
        result[0:tokens, pl.ds(first, GROUP)] = nt(grad_raised[...], up_rows)

    mark("raise_back")
    columns(groups, raise_back)

    sums[...] = jnp.zeros_like(sums)

    def second_back(at):
        normed, inverse = layer_norm(middle[at])
        through, total = norm_back(result[at], normed, inverse, gains[8:9])
        sums[8:16] += jnp.broadcast_to(total, (8, width))
        grad_middle = up_ref[at] + through
        up_ref[at] = grad_middle
        grad_low[at] = grad_middle.astype(BF16)

    mark("norm_two_back")
    by_rows(second_back)

    def split_columns(value):
        return value.reshape(p.rings, 2, 2, rows, value.shape[1])

    def project_back(first, number):
        grad = tn(attended[...], grad_low[:, pl.ds(first, GROUP)])
        scatter_up.put(across(pl.multiple_of(hid + first, GROUP), GROUP), split_columns(grad))
        share = p.rings // groups
        proj_rows = one[pl.ds(number * share, share), :, :, :, pl.ds(3 * width, width)]
        grad_attended[:, pl.ds(first, GROUP)] = nt(
            grad_low[...], proj_rows.reshape(GROUP, width)
        ).astype(BF16)

    mark("project_back")
    columns(groups, project_back)
    scatter_up.trade(across(hid, width), p.rings)

    def attend_back(group, turns, number, _):
        window = number
        at = pl.ds(pl.multiple_of(window * TOK, 16), TOK)
        query = packed[at, head_lanes(group * GROUP)]
        keyed = packed[at, head_lanes(width + group * GROUP)]
        valued = packed[at, head_lanes(2 * width + group * GROUP)]
        upstream = grad_attended[at, head_lanes(group * GROUP)]
        key_turned = jnp.transpose(keyed.astype(F32), (1, 0)).astype(BF16)
        grad_key = jnp.zeros((TOK, GROUP), F32)
        grad_value = jnp.zeros((TOK, GROUP), F32)
        parts = []
        for h in range(per):
            if h == per // 2:
                at_turn(number, turns, 0)
            probs = probs_ref[(number * groups + group) * per + h]
            mine = lanes == h
            grad_probs = nt(jnp.where(mine, valued, jnp.zeros_like(valued)), upstream)
            grad_value = jnp.where(mine, nn(probs.astype(BF16), upstream), grad_value)
            inner = jnp.sum(grad_probs * probs, axis=0, keepdims=True)
            grad_scores = (probs * (grad_probs - inner) * scale).astype(BF16)
            grad_key = jnp.where(mine, nn(grad_scores, query), grad_key)
            parts.append(nn(key_turned[h * head : (h + 1) * head], grad_scores))
        grad_query = jnp.transpose(jnp.concatenate(parts, axis=0), (1, 0))
        grad_packed[at, head_lanes(group * GROUP)] = grad_query.astype(BF16)
        grad_packed[at, head_lanes(width + group * GROUP)] = grad_key.astype(BF16)
        grad_packed[at, head_lanes(2 * width + group * GROUP)] = grad_value.astype(BF16)
        at_turn(number, turns, 1)
        return 0

    def pack_back(group):
        def run(part, _):
            first = pl.multiple_of(part * width + group * GROUP, GROUP)
            grad = tn(hidden_one[...], grad_packed[:, pl.ds(first, GROUP)])
            where = across(pl.multiple_of(part * GROUP, GROUP), GROUP)
            scatter_query[group].put(where, split_columns(grad))
            return 0

        lax.fori_loop(0, 2, run, 0)
        scatter_query[group].trade(full, 0)
        first = 2 * width + group * GROUP
        grad = tn(hidden_one[...], grad_packed[:, first : first + GROUP])
        scatter_value[group].put(across(0, GROUP), split_columns(grad))

    full = (every, every, every, every)

    def up_cross():
        scatter_up.traded(across(hid, width), p.rings)
        scatter_up.cross()

    def packed_cross(group):
        scatter_query[group].traded(full, 0)
        scatter_query[group].cross()
        scatter_value[group].traded(full, 0)
        scatter_value[group].cross()

    turns_one = [[] for _ in range(8)]
    turns_one[2].append(up_cross)
    turns_two = [[] for _ in range(8)]
    turns_two[1].append(scatter_down.crossed)
    turns_two[3].append(functools.partial(packed_cross, 0))

    mark("attend_back")
    lax.fori_loop(0, 4, functools.partial(attend_back, 0, turns_one), 0)
    mark("pack_back")
    pack_back(0)
    scatter_value[0].put(across(GROUP, GROUP), jnp.zeros((p.rings, 2, 2, rows, GROUP), F32))
    scatter_value[0].trade(full, 0)
    mark("attend_back_two")
    lax.fori_loop(0, 4, functools.partial(attend_back, 1, turns_two), 0)
    mark("pack_back_two")
    pack_back(1)
    scatter_up.crossed()

    def unpack(first, number):
        share = p.rings // groups
        rows_here = one[pl.ds(number * share, share), :, :, :, pl.ds(0, 3 * width)]
        result[0:tokens, pl.ds(first, GROUP)] = nt(
            grad_packed[...], rows_here.reshape(GROUP, 3 * width)
        )

    columns(groups, unpack)
    scatter_down.spread()

    def first_back(at):
        normed, inverse = layer_norm(x_ref[at])
        through, total = norm_back(result[at], normed, inverse, gains[0:1])
        sums[0:8] += jnp.broadcast_to(total, (8, width))
        up_ref[at] = up_ref[at] + through

    mark("norm_one_back")
    by_rows(first_back)
    line = lax.broadcasted_iota(jnp.int32, (128, width), 0)
    both = jnp.where(line < 64, sums[0:1], sums[8:9])
    gain_sums = jnp.transpose(both, (1, 0))
    gain_sums = jnp.concatenate([gain_sums, gain_sums], axis=1)
    scatter_value[1].put(across(GROUP, GROUP), split_columns(gain_sums))
    mark("trade_last")
    scatter_value[1].trade(full, 0)
    scatter_query[1].traded(full, 0)
    scatter_query[1].cross()
    send_back(up_ref, 1)
    scatter_value[1].traded(full, 0)
    scatter_value[1].cross()
    mark("last")
    for early in (scatter_query[0], scatter_value[0]):
        early.crossed()
    scatter_down.collect()
    scatter_up.spread()
    scatter_query[0].spread()
    scatter_value[0].spread()
    scatter_query[1].crossed()
    scatter_value[1].crossed()
    scatter_down.end()
    scatter_up.collect()
    scatter_query[0].collect()
    scatter_value[0].collect()
    scatter_query[1].spread()
    scatter_value[1].spread()
    scatter_up.end()
    scatter_query[0].end()
    scatter_value[0].end()

    def write_packed(group):
        here = group * GROUP
        value = scatter_query[group].columns()
        out_one[:, here : here + GROUP] = value[:, :GROUP]
        out_one[:, width + here : width + here + GROUP] = value[:, GROUP:]
        value = scatter_value[group].columns()
        out_one[:, 2 * width + here : 2 * width + here + GROUP] = value[:, :GROUP]
        if group == 1:
            out_one[:, 4 * width :] = value[:, GROUP : GROUP + 128]

    out_three[...] = scatter_down.columns()
    value = scatter_up.columns()
    out_two[...] = value[:, :hid]
    out_one[:, 3 * width : 4 * width] = value[:, hid:]
    write_packed(0)
    mark("collect_last")
    scatter_query[1].collect()
    scatter_value[1].collect()
    number = 0
    for i, j, window, quarter, down, over in shifted_blocks():
        if down or over:
            for kind in range(2):
                wires.landed(
                    out_field.at[(i + 1) % 4, (j + 1) % 4, kind],
                    returns + 7 * kind + number,
                    beyond(down, over, -1),
                )
            number += 1
    scatter_query[1].end()
    scatter_value[1].end()
    write_packed(1)
    mark("finish")
    wires.finish(p.sibling)
    mark()


def blocks_of(field):
    height, breadth, depth = field.shape
    shaped = field.reshape(height // SHIFT, SHIFT, breadth // SHIFT, SHIFT, depth)
    shaped = shaped.transpose(0, 2, 1, 3, 4).reshape(4, 4, QUAD, depth)
    return jnp.pad(shaped, ((0, 0), (0, 0), (0, PADQ - QUAD), (0, 0)))


def field_of(blocks):
    depth = blocks.shape[-1]
    shaped = blocks[:, :, :QUAD].reshape(4, 4, SHIFT, SHIFT, depth)
    return shaped.transpose(0, 2, 1, 3, 4).reshape(4 * SHIFT, 4 * SHIFT, depth)


def body(
    lats,
    lons,
    cells,
    cotangent,
    land,
    land_embed,
    qkv_weight,
    proj_weight,
    up_weight,
    down_weight,
    gain_one,
    gain_two,
):
    start = (
        cells.astype(F32) + land[:, :, None].astype(F32) * land_embed[None, None, :]
    ).astype(BF16)
    field = jnp.stack([blocks_of(start), blocks_of(cotangent)], axis=2)
    rows, hid = up_weight.shape
    width = cells.shape[2]
    deep = down_weight.shape[0]
    tokens = 4 * TOK
    rings = lons // 4
    shard_one = jnp.concatenate(
        [
            qkv_weight,
            proj_weight,
            jnp.broadcast_to(gain_one[:, None], (rows, 64)),
            jnp.broadcast_to(gain_two[:, None], (rows, 64)),
        ],
        axis=1,
    )

    def scatter_scratch(lines, across):
        quarter = across // 4
        return [
            pltpu.VMEM((rings, 2, lines, across), F32),
            pltpu.VMEM((rings, 2, lines, across), BF16),
            pltpu.VMEM((rings, 2, lines, across), BF16),
            pltpu.VMEM((3, rings, 2, lines, quarter), BF16),
            pltpu.VMEM((3, rings, 2, lines, quarter), BF16),
            pltpu.VMEM((rings, 2, lines, quarter), F32),
            pltpu.VMEM((rings - 1, 2, lines, quarter), BF16),
            pltpu.VMEM((rings - 1, 2, lines, quarter), BF16),
            pltpu.VMEM((2, lines, quarter), F32),
            pltpu.VMEM((4, 2, lines, quarter), F32),
            pltpu.VMEM((4, lines, quarter), F32),
        ]

    scratch = [
        pltpu.VMEM((4, 4, 2, PADQ, width), BF16),
        pltpu.VMEM((7, 2, PADQ, width), BF16),
        pltpu.VMEM((tokens + 16, width), F32),
        pltpu.VMEM((tokens + 16, width), F32),
        pltpu.VMEM((tokens, width), BF16),
        pltpu.VMEM((tokens, width), BF16),
        pltpu.VMEM((tokens, 3 * width), BF16),
        pltpu.VMEM((4 * HEADS, TOK, TOK), F32),
        pltpu.VMEM((tokens, width), BF16),
        pltpu.VMEM((tokens, width), F32),
        pltpu.VMEM((tokens + 16, width), F32),
        pltpu.VMEM((tokens, width), BF16),
        pltpu.VMEM((tokens, hid), BF16),
        pltpu.VMEM((tokens, hid), BF16),
        pltpu.VMEM((tokens, width), BF16),
        pltpu.VMEM((tokens, width), BF16),
        pltpu.VMEM((tokens, 3 * width), BF16),
        pltpu.VMEM((16, width), F32),
        pltpu.VMEM((16, width), F32),
        pltpu.VMEM((rings, 2, 2, rows, 4 * width + 128), BF16),
        pltpu.VMEM((rings, 2, 2, rows, hid), BF16),
        pltpu.VMEM((rings, 2, 2, deep, width), BF16),
    ]
    scratch += scatter_scratch(deep, width)
    scratch += scatter_scratch(rows, hid + width)
    for _ in range(4):
        scratch += scatter_scratch(rows, 2 * GROUP)
    wires = 14 + 14 + 3 * (3 * rings - 1) + 6 * (rings - 1 + 9) + 2 * rings + 5
    scratch += [pltpu.SemaphoreType.DMA((wires,)), pltpu.SemaphoreType.DMA((wires,))]
    vmem = pl.BlockSpec(memory_space=pltpu.VMEM)
    out_field, one, two, three = pl.pallas_call(
        functools.partial(kernel, lats, lons),
        out_shape=(
            jax.ShapeDtypeStruct((4, 4, 2, PADQ, width), BF16),
            jax.ShapeDtypeStruct((rows, 4 * width + 128), F32),
            jax.ShapeDtypeStruct((rows, hid), F32),
            jax.ShapeDtypeStruct((deep, width), F32),
        ),
        in_specs=[vmem] * 4,
        out_specs=(vmem,) * 4,
        scratch_shapes=scratch,
        compiler_params=pltpu.CompilerParams(
            collective_id=0, has_side_effects=True, vmem_limit_bytes=63 * 2**20
        ),
        name="block",
    )(field, shard_one, up_weight, down_weight)
    return (
        field_of(out_field[:, :, 0]),
        field_of(out_field[:, :, 1]),
        one[:, : 3 * width],
        one[:, 3 * width : 4 * width],
        two,
        three,
        one[:, 4 * width],
        one[:, 4 * width + 64],
    )


def solution(mesh):
    placed = (
        P("lat", "lon", None),
        P("lat", "lon", None),
        P("lat", "lon"),
        P(),
        P("lon", None),
        P("lon", None),
        P("lon", None),
        P("lon", None),
        P("lon"),
        P("lon"),
    )
    return jax.shard_map(
        functools.partial(body, mesh.shape["lat"], mesh.shape["lon"]),
        mesh=mesh,
        in_specs=placed,
        out_specs=(
            P("lat", "lon", None),
            P("lat", "lon", None),
            P("lon", None),
            P("lon", None),
            P("lon", None),
            P("lon", None),
            P("lon"),
            P("lon"),
        ),
        check_vma=False,
    )
```

```python
import functools

import jax
import jax.numpy as jnp
from jax import lax
from jax.experimental import pallas as pl
from jax.experimental.pallas import tpu as pltpu
from jax.sharding import PartitionSpec as P

HEADS = 16
WIN = 12
SHIFT = 6
EPS = 1e-5
NEG = -1e30
TOK = WIN * WIN
QUAD = SHIFT * SHIFT
PADQ = 48
GROUP = 256
F32 = jnp.float32
BF16 = jnp.bfloat16
MESH = pl.DeviceIdType.MESH


def nn(a, b):
    return lax.dot_general(a, b, (((1,), (0,)), ((), ())), preferred_element_type=F32)


def nt(a, b):
    return lax.dot_general(a, b, (((1,), (1,)), ((), ())), preferred_element_type=F32)


def tn(a, b):
    return lax.dot_general(a, b, (((0,), (0,)), ((), ())), preferred_element_type=F32)


def layer_norm(x):
    centred = x - jnp.mean(x, axis=-1, keepdims=True)
    spread = jnp.mean(centred * centred, axis=-1, keepdims=True)
    inverse = lax.rsqrt(spread + EPS)
    return centred * inverse, inverse


def norm_back(upstream, normed, inverse, gain):
    scaled = upstream * gain
    inner = (
        scaled
        - jnp.mean(scaled, axis=-1, keepdims=True)
        - normed * jnp.mean(scaled * normed, axis=-1, keepdims=True)
    )
    return inner * inverse, jnp.sum(upstream * normed, axis=0, keepdims=True)


class Marks:
    def __init__(self):
        self.open = None

    def __call__(self, name=None):
        if self.open is not None:
            self.open.__exit__(None, None, None)
        self.open = None
        if name is not None:
            self.open = jax.named_scope(name)
            self.open.__enter__()


class Place:
    def __init__(self, lats, lons):
        self.lats, self.lons, self.rings = lats, lons, lons // 4
        self.lat = lax.axis_index("lat")
        self.lon = lax.axis_index("lon")
        self.z = self.lon // 4
        self.yh = (self.lon // 2) % 2
        self.core = self.lon % 2
        self.sibling = (self.lat, self.lon + 1 - 2 * self.core)
        near = self.lat + 1 - 2 * (self.lat % 2)
        self.partner = (near, self.z * 4 + (1 - self.yh) * 2 + self.core)

        self.zs = [self.z] + [(self.z + by) % self.rings for by in range(1, self.rings)]
        side = self.yh * 2 + self.core
        self.on_z = [(self.lat, z * 4 + side) for z in self.zs]
        steps = ((0, 1), (1, 0), (1, 1))
        self.around = {}
        for by_lat, by_lon in steps:
            ahead = ((self.lat + by_lat) % lats, (self.lon + by_lon) % lons)
            behind = ((self.lat - by_lat + lats) % lats, (self.lon - by_lon + lons) % lons)
            self.around[by_lat, by_lon] = ahead
            self.around[-by_lat, -by_lon] = behind
        self.size = {"x": lats // 2, "y": 4}
        x, low = self.lat // 2, self.lat % 2
        xs = [x] + [(x + by) % (lats // 2) for by in range(1, lats // 2)]
        y = self.yh * 2 + low
        ys = [y] + [(y + by) % 4 for by in range(1, 4)]
        here = self.z * 4 + self.core
        self.on = {
            "x": [(number, (number * 2 + low, self.lon)) for number in xs],
            "y": [(number, (x * 2 + number % 2, here + number // 2 * 2)) for number in ys],
        }

    def z_of(self, by):
        return self.zs[by % self.rings]

    def along_z(self, by):
        return self.on_z[by % self.rings]

    def moved(self, by_lat, by_lon):
        return self.around[by_lat, by_lon]

    def at(self, axis, by):
        return self.on[axis][by % self.size[axis]]


class Wires:
    def __init__(self, send, recv):
        self.send, self.recv, self.used, self.sent = send, recv, 0, []

    def take(self, count):
        first = self.used
        self.used += count
        return first

    def copy(self, src, dst, index, device):
        return pltpu.make_async_remote_copy(
            src_ref=src,
            dst_ref=dst,
            send_sem=self.send.at[index],
            recv_sem=self.recv.at[index],
            device_id=device,
            device_id_type=MESH,
        )

    def start(self, src, dst, index, device, until=None):
        self.copy(src, dst, index, device).start()
        if until is not None:
            self.sent.append((until, index))

    def landed(self, ref, index, device):
        self.copy(ref, ref, index, device).wait_recv()

    def finish(self, device):
        for view, index in self.sent:
            ref = view()
            self.copy(ref, ref, index, device).wait_send()


class Gather:
    def __init__(self, place, wires, shard, whole):
        self.p, self.w, self.shard, self.whole = place, wires, shard, whole
        self.half = place.rings // 2
        self.last = 2 * self.half
        self.far = wires.take(1)
        self.way = {1: wires.take(self.last - 1), -1: wires.take(self.last - 1)}
        self.side = wires.take(place.rings)

    def slot(self, rel, other):
        p = self.p
        yh = 1 - p.yh if other else p.yh
        return self.whole.at[p.z_of(-rel), yh, p.core]

    def pair(self, rel, core):
        p = self.p
        return self.whole.at[p.z_of(-rel), :, core]

    def forward(self, way, hop, other):
        if hop == self.half - 1 and other != (way < 0):
            return
        index = self.way[way] + (2 * hop + other if hop < self.half - 1 else 2 * hop)
        block = self.slot(way * hop, other)
        self.w.start(block, block, index, self.p.along_z(way), lambda: self.whole.at[0, 0, 0])

    def landed(self, way, hop, other):
        index = self.way[way] + (2 * (hop - 1) + other if hop < self.half else 2 * (hop - 1))
        self.w.landed(self.slot(way * hop, other), index, self.p.along_z(-way))

    def share(self, rel):
        p = self.p
        index = self.side + rel % p.rings
        block = self.pair(rel, p.core)
        self.w.start(block, block, index, p.sibling, lambda: self.whole.at[0, :, 0])

    def tick(self, step):
        p = self.p
        if step == 0:
            here = self.slot(0, 0)
            here[...] = self.shard[...]
            for way in (1, -1):
                self.forward(way, 0, 0)
            self.w.start(self.shard, here, self.far, p.partner, lambda: self.shard)
        elif step == 1:
            self.w.landed(self.slot(0, 1), self.far, p.partner)
            for way in (1, -1):
                self.forward(way, 0, 1)
            self.share(0)
        elif step < self.last:
            hop, other = step // 2, step % 2
            for way in (1, -1):
                self.landed(way, hop, other)
                self.forward(way, hop, other)
            if other:
                for way in (1, -1):
                    self.share(way * hop)
        else:
            self.landed(1, self.half, 0)
            self.landed(-1, self.half, 1)
            self.share(self.half)

    def end(self):
        p = self.p
        for rel in range(p.rings):
            self.w.landed(self.pair(rel, 1 - p.core), self.side + rel, p.sibling)


class Quarters(Gather):
    def __init__(self, place, wires, shard, whole, axis):
        super().__init__(place, wires, shard, whole)
        self.axis = axis
        self.size = place.size[axis]
        self.count = shard.shape[1] // self.size
        self.over = wires.take(self.size - 1)
        self.mine = self.span(self.p.at(axis, 0)[0])
        partner = place.partner[0] % 2 + 2 * (1 - place.yh) if axis == "y" else place.lat // 2
        self.theirs = self.span(partner)

    def span(self, number):
        return pl.ds(pl.multiple_of(number * self.count, 128), self.count)

    def slot(self, rel, other):
        p = self.p
        yh = 1 - p.yh if other else p.yh
        return self.whole.at[p.z_of(-rel), yh, p.core, :, self.mine]

    def all_of(self, core, by):
        return self.whole.at[:, :, core, :, self.span(self.p.at(self.axis, by)[0])]

    def forward(self, way, hop, other):
        if hop == self.half - 1 and other != (way < 0):
            return
        index = self.way[way] + (2 * hop + other if hop < self.half - 1 else 2 * hop)
        block = self.slot(way * hop, other)
        self.w.start(block, block, index, self.p.along_z(way), lambda: self.slot(0, 0))

    def share(self, rel):
        pass

    def begin(self):
        p = self.p
        self.whole[p.z, p.yh, p.core, :, self.mine] = self.shard[:, self.mine]
        for way in (1, -1):
            self.forward(way, 0, 0)
        self.w.start(
            self.shard.at[:, self.theirs],
            self.whole.at[p.z, p.yh, p.core, :, self.theirs],
            self.far,
            p.partner,
            lambda: self.shard.at[:, self.mine],
        )

    def tick(self, step):
        if step == 0:
            self.begin()
        else:
            super().tick(step)

    def view(self):
        return self.all_of(self.p.core, 0)

    def exchange(self):
        block = self.view()
        self.w.start(block, block, self.side, self.p.sibling, self.view)
        for by in range(1, self.size):
            device = self.p.at(self.axis, by)[1]
            self.w.start(block, block, self.over + by - 1, device, self.view)

    def arrive(self):
        for by in range(1, self.size):
            block = self.all_of(self.p.core, -by)
            self.w.landed(block, self.over + by - 1, self.p.at(self.axis, -by)[1])
            self.w.start(block, block, self.side + by, self.p.sibling, self.view)

    def end(self):
        for by in range(self.size):
            self.w.landed(self.all_of(1 - self.p.core, -by), self.side + by, self.p.sibling)


class Scatter:
    def __init__(self, place, wires, refs, pieces, axis):
        self.p, self.w, self.pieces, self.axis = place, wires, pieces, axis
        self.own, self.away, self.near, self.give, self.got, self.sum = refs[:6]
        self.out, self.into, self.stage, self.land, self.full = refs[6:]
        self.size = place.size
        self.other = "y" if axis == "x" else "x"
        self.count = self.sum.shape[3]
        self.exchange = wires.take(pieces)
        self.over = wires.take(3)
        self.ring = wires.take(place.rings - 1)
        self.plane = wires.take(3)
        self.along = wires.take(3)

    def put(self, where, value):
        first, second = value[..., 0, :, :], value[..., 1, :, :]
        mine = self.p.core == 0
        self.own[where] = jnp.where(mine, first, second)
        self.away[where] = jnp.where(mine, second, first).astype(BF16)

    def trade(self, where, index):
        self.w.copy(
            self.away.at[where], self.near.at[where], self.exchange + index, self.p.sibling
        ).start()

    def traded(self, where, index):
        copy = self.w.copy(
            self.away.at[where], self.near.at[where], self.exchange + index, self.p.sibling
        )
        copy.wait_send()
        copy.wait_recv()

    def at(self, axis, by):
        return self.p.at(axis, by)

    def quarter(self, number):
        every = slice(None)
        first = pl.multiple_of(number * self.count, 128)
        at = (every, every, every, pl.ds(first, self.count))
        return self.own[at] + self.near[at].astype(F32)

    def cross(self):
        for by in range(1, self.size[self.axis]):
            number, device = self.at(self.axis, by)
            self.give[by - 1] = self.quarter(number).astype(BF16)
            source = self.give.at[by - 1]
            self.w.start(
                source, self.got.at[by - 1], self.over + by - 1, device, lambda: self.give.at[0]
            )

    def crossed(self):
        p = self.p
        total = self.quarter(self.at(self.axis, 0)[0])
        for by in range(1, self.size[self.axis]):
            device = self.at(self.axis, -by)[1]
            self.w.landed(self.got.at[by - 1], self.over + by - 1, device)
            total = total + self.got[by - 1].astype(F32)
        self.sum[...] = total
        for by in range(1, p.rings):
            self.out[by - 1] = self.sum[p.z_of(by)].astype(BF16)
            source = self.out.at[by - 1]
            self.w.start(
                source,
                self.into.at[by - 1],
                self.ring + by - 1,
                p.along_z(by),
                lambda: self.out.at[0],
            )

    def spread(self):
        p = self.p
        total = self.sum[p.z]
        for by in range(1, p.rings):
            self.w.landed(self.into.at[by - 1], self.ring + by - 1, p.along_z(-by))
            total = total + self.into[by - 1].astype(F32)
        self.stage[...] = total
        here = self.at(self.other, 0)[0]
        self.land[here] = self.stage[...]
        for by in range(1, self.size[self.other]):
            device = self.at(self.other, by)[1]
            self.w.start(
                self.stage,
                self.land.at[here],
                self.plane + by - 1,
                device,
                lambda: self.land.at[0],
            )

    def collect(self):
        p = self.p
        size = self.size[self.other]
        for by in range(1, size):
            number, device = self.at(self.other, -by)
            self.w.landed(self.land.at[number], self.plane + by - 1, device)
        total = self.land[0]
        for number in range(1, size):
            total = total + self.land[number]
        mine = self.at(self.other, 0)[0]
        self.land[mine] = total
        here = self.at(self.axis, 0)[0]
        self.full[here] = self.land[mine, p.yh]
        for by in range(1, self.size[self.axis]):
            number, device = self.at(self.axis, by)
            yh = p.yh if self.axis == "x" else number // 2
            self.w.start(
                self.land.at[mine, yh],
                self.full.at[here],
                self.along + by - 1,
                device,
                lambda: self.full.at[0],
            )

    def end(self):
        for by in range(1, self.size[self.axis]):
            number, device = self.at(self.axis, -by)
            self.w.landed(self.full.at[number], self.along + by - 1, device)

    def columns(self):
        return jnp.concatenate(
            [self.full[number] for number in range(self.size[self.axis])], axis=1
        )


def shifted_blocks():
    for window in range(4):
        for quarter in range(4):
            i = 2 * (window // 2) + quarter // 2
            j = 2 * (window % 2) + quarter % 2
            yield i, j, window, quarter, i == 3, j == 3


def kernel(
    lats,
    lons,
    cells_in,
    cotangent_in,
    qkv_shard,
    proj_shard,
    gain_shard,
    shard_two,
    shard_three,
    out_block,
    out_grad,
    out_one,
    out_two,
    out_three,
    moved,
    back,
    x_ref,
    up_ref,
    low_up,
    hidden_one,
    packed,
    probs_ref,
    attended,
    middle,
    result,
    hidden_two,
    active,
    grad_raised,
    grad_attended,
    grad_low,
    grad_packed,
    gains,
    sums,
    shard_one,
    one,
    two,
    three,
    *rest,
):
    scatter_refs, (send_sem, recv_sem) = rest[:-2], rest[-2:]
    p = Place(lats, lons)
    wires = Wires(send_sem, recv_sem)
    width = x_ref.shape[1]
    hid = shard_two.shape[1]
    chunk = hid // p.rings
    rows = width // lons
    tokens = 4 * TOK
    scale = (width // HEADS) ** -0.5
    per = GROUP * HEADS // width
    head = width // HEADS
    groups = width // GROUP

    mark = Marks()
    mark("barrier")
    shard_one[:, : 3 * width] = qkv_shard[...]
    shard_one[:, 3 * width : 4 * width] = proj_shard[...]
    shard_one[:, 4 * width :] = gain_shard[...]
    barrier = pltpu.get_barrier_semaphore()
    friends = [p.sibling] + [p.along_z(by) for by in range(1, p.rings)]
    friends += [p.at(axis, by)[1] for axis in ("x", "y") for by in range(1, p.size[axis])]
    for by_lat, by_lon in ((1, 0), (0, 1), (1, 1)):
        friends += [p.moved(by_lat, by_lon), p.moved(-by_lat, -by_lon)]
    for friend in friends:
        pl.semaphore_signal(barrier, inc=1, device_id=friend, device_id_type=MESH)
    pl.semaphore_wait(barrier, len(friends))

    def beyond(by_rows, by_columns, sign):
        return p.moved(sign * int(by_rows), sign * int(by_columns))

    mark("gather_one")
    halo = wires.take(14)
    fields, outs = (cells_in, cotangent_in), (out_block, out_grad)
    edge = [item for item in shifted_blocks() if item[4] or item[5]]
    first_weight = Gather(p, wires, shard_one, one)
    second_weight = Quarters(p, wires, shard_two, two, "x")
    third_weight = Quarters(p, wires, shard_three, three, "y")

    def send_halo(kind):
        for number, (i, j, window, quarter, down, over) in enumerate(edge):
            wires.start(
                fields[kind].at[(i + 1) % 4, (j + 1) % 4],
                moved.at[window, quarter, kind],
                halo + 7 * kind + number,
                beyond(down, over, -1),
                lambda: moved.at[0, 0, 0],
            )

    def assemble(kind, windows, target):
        numbers = {item[2:4]: number for number, item in enumerate(edge)}
        for i, j, window, quarter, down, over in shifted_blocks():
            if window not in windows:
                continue
            if down or over:
                wires.landed(
                    moved.at[window, quarter, kind],
                    halo + 7 * kind + numbers[(window, quarter)],
                    beyond(down, over, 1),
                )
                block = moved[window, quarter, kind]
            else:
                block = fields[kind][i + 1, j + 1]
            target[pl.ds(TOK * window + QUAD * quarter, PADQ)] = block.astype(F32)

    first_weight.tick(0)
    send_halo(0)
    second_weight.tick(0)
    third_weight.tick(0)
    for step in range(1, first_weight.last + 1):
        first_weight.tick(step)
        second_weight.tick(step)
        third_weight.tick(step)
    second_weight.exchange()
    third_weight.exchange()
    send_halo(1)
    mark("gather_one_end")
    first_weight.end()
    assemble(0, (0, 1, 2, 3), x_ref)

    def weight(ref, first, count):
        return ref[:, :, :, :, pl.ds(first, count)].reshape(width, count)

    mark("norm_one")
    turned = jnp.transpose(weight(one, 4 * width, 128).astype(F32), (1, 0))
    gains[0:8] = jnp.broadcast_to(turned[0:1], (8, width))
    gains[8:16] = jnp.broadcast_to(turned[64:65], (8, width))

    def by_rows(body):
        def run(window, _):
            body(pl.ds(pl.multiple_of(window * TOK, 16), TOK))
            return 0

        lax.fori_loop(0, 4, run, 0)

    def first_norm(at):
        normed, _ = layer_norm(x_ref[at])
        hidden_one[at] = (normed * gains[0:1]).astype(BF16)

    by_rows(first_norm)

    def columns(count, body):
        def run(number, _):
            body(pl.multiple_of(number * GROUP, GROUP), number)
            return 0

        lax.fori_loop(0, count, run, 0)

    def pack(first, number):
        packed[:, pl.ds(first, GROUP)] = nn(hidden_one[...], weight(one, first, GROUP)).astype(
            BF16
        )

    mark("qkv")
    columns(3 * groups, pack)

    mark("attend")
    lanes = lax.broadcasted_iota(jnp.int32, (TOK, GROUP), 1) // head
    late = lax.broadcasted_iota(jnp.int32, (TOK, TOK), 0) >= TOK // 2
    late_query = lax.broadcasted_iota(jnp.int32, (TOK, TOK), 1) >= TOK // 2
    differ = late != late_query

    def head_lanes(first):
        return pl.ds(pl.multiple_of(first, GROUP), GROUP)

    def at_turn(number, turns, turn_of):
        for turn in range(turn_of, len(turns), 2):
            if turns[turn]:

                def act(turn=turn):
                    for action in turns[turn]:
                        action()

                pl.when(number == turn // 2)(act)

    turns = [[] for _ in range(8 * groups)]
    turns[14].append(second_weight.arrive)
    turns[15].append(third_weight.arrive)

    def attend(number, _):
        window, group = number // groups, number % groups
        at = pl.ds(pl.multiple_of(window * TOK, 16), TOK)
        query = packed[at, head_lanes(group * GROUP)]
        keyed = packed[at, head_lanes(width + group * GROUP)]
        valued = packed[at, head_lanes(2 * width + group * GROUP)]
        split = jnp.logical_and(p.lat == lats - 1, window >= 2)
        bias = jnp.where(jnp.logical_and(differ, split), NEG, 0.0)
        value_turned = jnp.transpose(valued.astype(F32), (1, 0)).astype(BF16)
        parts = []
        for h in range(per):
            if h == per // 2:
                at_turn(number, turns, 0)
            mine = jnp.where(lanes == h, keyed, jnp.zeros_like(keyed))
            scores = nt(mine, query) * scale + bias
            raised = jnp.exp(scores - jnp.max(scores, axis=0, keepdims=True))
            probs = raised * (1.0 / jnp.sum(raised, axis=0, keepdims=True))
            probs_ref[number * per + h] = probs
            parts.append(nn(value_turned[h * head : (h + 1) * head], probs.astype(BF16)))
        attended[at, head_lanes(group * GROUP)] = jnp.transpose(
            jnp.concatenate(parts, axis=0), (1, 0)
        ).astype(BF16)
        at_turn(number, turns, 1)
        return 0

    lax.fori_loop(0, 4 * groups, attend, 0)
    mark("project")

    def project(first, number):
        middle[:, pl.ds(first, GROUP)] = x_ref[0:tokens, pl.ds(first, GROUP)] + nn(
            attended[...], weight(one, pl.multiple_of(3 * width + first, GROUP), GROUP)
        )

    columns(groups, project)
    assemble(1, (0, 1, 2, 3), up_ref)

    def second_norm(at):
        normed, _ = layer_norm(middle[at])
        hidden_two[at] = (normed * gains[8:9]).astype(BF16)
        low_up[at] = up_ref[at].astype(BF16)

    by_rows(second_norm)
    mark("gather_end")
    second_weight.end()
    third_weight.end()

    def scatter(number, pieces, axis):
        return Scatter(p, wires, scatter_refs[11 * number : 11 * number + 11], pieces, axis)

    scatter_down = scatter(0, p.rings, "y")
    scatter_up = scatter(1, p.rings, "x")
    scatter_proj = scatter(6, 1, "x")
    scatter_query = [scatter(2, 1, "y"), scatter(3, 1, "x")]
    scatter_value = [scatter(4, 1, "x"), scatter(5, 1, "y")]
    every = slice(None)

    def across(first, count):
        return (every, every, every, pl.ds(first, count))

    def ring_place(rel):
        return (p.z + rel + p.rings) % p.rings

    def feed(number, _):
        rel = jnp.where(
            number % 2 == 1, p.rings // 2 - (number + 1) // 2, p.rings // 2 + number // 2
        )
        place = ring_place(rel)
        first = pl.ds(pl.multiple_of(place * chunk, 128), chunk)
        up_weight = two[:, :, :, :, first].reshape(width, chunk)
        raised_up = nn(hidden_two[...], up_weight)
        share = 0.5 * (1.0 + lax.erf(raised_up * 0.7071067811865476))
        act = (raised_up * share).astype(BF16)
        active[:, first] = act
        slope = share + raised_up * jnp.exp(-0.5 * raised_up * raised_up) * 0.3989422804014327
        grad_down = tn(act, low_up[...])
        scatter_down.put((place,), grad_down.reshape(2, 2, chunk // 4, width))
        scatter_down.trade((place,), place)
        down_weight = three[place].reshape(chunk, width)
        grads = (nt(low_up[...], down_weight) * slope).astype(BF16)
        grad_raised[:, first] = grads
        grad_up = tn(hidden_two[...], grads)
        where = across(pl.multiple_of(place * chunk, 128), chunk)
        scatter_up.put(where, grad_up.reshape(p.rings, 2, 2, rows, chunk))
        scatter_up.trade(where, place)
        return 0

    mark("feed")
    lax.fori_loop(0, p.rings, feed, 0)

    def lower(first, number):
        down = three[:, :, :, :, pl.ds(first, GROUP)].reshape(hid, GROUP)
        result[0:tokens, pl.ds(first, GROUP)] = middle[:, pl.ds(first, GROUP)] + nn(
            active[...], down
        )

    def trade_all(number, _):
        scatter_down.traded((number,), number)
        scatter_up.traded(across(pl.multiple_of(number * chunk, 128), chunk), number)
        return 0

    mark("lower")
    columns(groups, lower)

    returns = wires.take(14)

    def send_back(source, kind):
        number = 0
        for i, j, window, quarter, down, over in shifted_blocks():
            first = TOK * window + QUAD * quarter
            block = source[pl.ds(first, PADQ)].astype(BF16)
            target = outs[kind].at[(i + 1) % 4, (j + 1) % 4]
            if down or over:
                place = back.at[number, kind]
                place[...] = block
                index = returns + 7 * kind + number
                wires.start(place, target, index, beyond(down, over, 1), lambda: back.at[0, 0])
                number += 1
            else:
                target[...] = block

    mark("return_out")
    send_back(result, 0)
    lax.fori_loop(0, p.rings, trade_all, 0)
    scatter_down.cross()
    scatter_up.cross()

    def raise_back(first, number):
        share = p.rings // groups
        up_rows = two[pl.ds(number * share, share)].reshape(GROUP, hid)
        result[0:tokens, pl.ds(first, GROUP)] = nt(grad_raised[...], up_rows)

    mark("raise_back")
    columns(groups, raise_back)

    sums[...] = jnp.zeros_like(sums)

    def second_back(at):
        normed, inverse = layer_norm(middle[at])
        through, total = norm_back(result[at], normed, inverse, gains[8:9])
        sums[8:16] += jnp.broadcast_to(total, (8, width))
        grad_middle = up_ref[at] + through
        up_ref[at] = grad_middle
        grad_low[at] = grad_middle.astype(BF16)

    mark("norm_two_back")
    by_rows(second_back)

    def split_columns(value):
        return value.reshape(p.rings, 2, 2, rows, value.shape[1])

    def project_back(first, number):
        grad = tn(attended[...], grad_low[:, pl.ds(first, GROUP)])
        scatter_proj.put(across(first, GROUP), split_columns(grad))
        share = p.rings // groups
        proj_rows = one[pl.ds(number * share, share), :, :, :, pl.ds(3 * width, width)]
        grad_attended[:, pl.ds(first, GROUP)] = nt(
            grad_low[...], proj_rows.reshape(GROUP, width)
        ).astype(BF16)

    mark("project_back")
    columns(groups, project_back)
    full = (every, every, every, every)
    scatter_proj.trade(full, 0)

    def attend_back(group, turns, number, _):
        window = number
        at = pl.ds(pl.multiple_of(window * TOK, 16), TOK)
        query = packed[at, head_lanes(group * GROUP)]
        keyed = packed[at, head_lanes(width + group * GROUP)]
        valued = packed[at, head_lanes(2 * width + group * GROUP)]
        upstream = grad_attended[at, head_lanes(group * GROUP)]
        key_turned = jnp.transpose(keyed.astype(F32), (1, 0)).astype(BF16)
        grad_key = jnp.zeros((TOK, GROUP), F32)
        grad_value = jnp.zeros((TOK, GROUP), F32)
        parts = []
        for h in range(per):
            if h == per // 2:
                at_turn(number, turns, 0)
            probs = probs_ref[(number * groups + group) * per + h]
            mine = lanes == h
            grad_probs = nt(jnp.where(mine, valued, jnp.zeros_like(valued)), upstream)
            grad_value = jnp.where(mine, nn(probs.astype(BF16), upstream), grad_value)
            inner = jnp.sum(grad_probs * probs, axis=0, keepdims=True)
            grad_scores = (probs * (grad_probs - inner) * scale).astype(BF16)
            grad_key = jnp.where(mine, nn(grad_scores, query), grad_key)
            parts.append(nn(key_turned[h * head : (h + 1) * head], grad_scores))
        grad_query = jnp.transpose(jnp.concatenate(parts, axis=0), (1, 0))
        grad_packed[at, head_lanes(group * GROUP)] = grad_query.astype(BF16)
        grad_packed[at, head_lanes(width + group * GROUP)] = grad_key.astype(BF16)
        grad_packed[at, head_lanes(2 * width + group * GROUP)] = grad_value.astype(BF16)
        at_turn(number, turns, 1)
        return 0

    def pack_back(group):
        def run(part, _):
            first = pl.multiple_of(part * width + group * GROUP, GROUP)
            grad = tn(hidden_one[...], grad_packed[:, pl.ds(first, GROUP)])
            where = across(pl.multiple_of(part * GROUP, GROUP), GROUP)
            scatter_query[group].put(where, split_columns(grad))
            return 0

        lax.fori_loop(0, 2, run, 0)
        scatter_query[group].trade(full, 0)
        first = 2 * width + group * GROUP
        grad = tn(hidden_one[...], grad_packed[:, first : first + GROUP])
        scatter_value[group].put(across(0, GROUP), split_columns(grad))

    def proj_cross():
        scatter_proj.traded(full, 0)
        scatter_proj.cross()

    def packed_cross(group):
        scatter_query[group].traded(full, 0)
        scatter_query[group].cross()
        scatter_value[group].traded(full, 0)
        scatter_value[group].cross()

    turns_one = [[] for _ in range(8)]
    turns_one[2].append(proj_cross)
    turns_two = [[] for _ in range(8)]
    turns_two[0].append(scatter_down.crossed)
    turns_two[1].append(scatter_up.crossed)
    turns_two[5].append(scatter_proj.crossed)
    turns_two[3].append(functools.partial(packed_cross, 0))

    mark("attend_back")
    lax.fori_loop(0, 4, functools.partial(attend_back, 0, turns_one), 0)
    mark("pack_back")
    pack_back(0)
    scatter_value[0].put(across(GROUP, GROUP), jnp.zeros((p.rings, 2, 2, rows, GROUP), F32))
    scatter_value[0].trade(full, 0)
    mark("attend_back_two")
    lax.fori_loop(0, 4, functools.partial(attend_back, 1, turns_two), 0)
    mark("pack_back_two")
    pack_back(1)
    scatter_down.spread()
    for early in (scatter_query[0], scatter_value[0]):
        early.crossed()

    def unpack(first, number):
        share = p.rings // groups
        rows_here = one[pl.ds(number * share, share), :, :, :, pl.ds(0, 3 * width)]
        result[0:tokens, pl.ds(first, GROUP)] = nt(
            grad_packed[...], rows_here.reshape(GROUP, 3 * width)
        )

    columns(groups, unpack)

    def first_back(at):
        normed, inverse = layer_norm(x_ref[at])
        through, total = norm_back(result[at], normed, inverse, gains[0:1])
        sums[0:8] += jnp.broadcast_to(total, (8, width))
        up_ref[at] = up_ref[at] + through

    mark("norm_one_back")
    by_rows(first_back)
    line = lax.broadcasted_iota(jnp.int32, (128, width), 0)
    both = jnp.where(line < 64, sums[0:1], sums[8:9])
    gain_sums = jnp.transpose(both, (1, 0))
    gain_sums = jnp.concatenate([gain_sums, gain_sums], axis=1)
    scatter_value[1].put(across(GROUP, GROUP), split_columns(gain_sums))
    mark("trade_last")
    scatter_value[1].trade(full, 0)
    scatter_query[1].traded(full, 0)
    scatter_query[1].cross()
    send_back(up_ref, 1)
    scatter_value[1].traded(full, 0)
    scatter_value[1].cross()
    mark("last")
    scatter_up.spread()
    scatter_proj.spread()
    scatter_down.collect()
    scatter_query[0].spread()
    scatter_value[0].spread()
    scatter_query[1].crossed()
    scatter_value[1].crossed()
    scatter_down.end()
    scatter_up.collect()
    scatter_proj.collect()
    scatter_query[0].collect()
    scatter_value[0].collect()
    scatter_query[1].spread()
    scatter_value[1].spread()
    scatter_up.end()
    scatter_proj.end()
    scatter_query[0].end()
    scatter_value[0].end()

    def write_packed(group):
        here = group * GROUP
        value = scatter_query[group].columns()
        out_one[:, here : here + GROUP] = value[:, :GROUP]
        out_one[:, width + here : width + here + GROUP] = value[:, GROUP:]
        value = scatter_value[group].columns()
        out_one[:, 2 * width + here : 2 * width + here + GROUP] = value[:, :GROUP]
        if group == 1:
            out_one[:, 4 * width :] = value[:, GROUP : GROUP + 128]

    out_three[...] = scatter_down.columns()
    out_two[...] = scatter_up.columns()
    out_one[:, 3 * width : 4 * width] = scatter_proj.columns()
    write_packed(0)
    mark("collect_last")
    scatter_query[1].collect()
    scatter_value[1].collect()
    number = 0
    for i, j, window, quarter, down, over in shifted_blocks():
        if down or over:
            for kind in range(2):
                wires.landed(
                    outs[kind].at[(i + 1) % 4, (j + 1) % 4],
                    returns + 7 * kind + number,
                    beyond(down, over, -1),
                )
            number += 1
    scatter_query[1].end()
    scatter_value[1].end()
    write_packed(1)
    mark("finish")
    wires.finish(p.sibling)
    mark()


def blocks_of(field):
    height, breadth, depth = field.shape
    shaped = field.reshape(height // SHIFT, SHIFT, breadth // SHIFT, SHIFT, depth)
    shaped = shaped.transpose(0, 2, 1, 3, 4).reshape(4, 4, QUAD, depth)
    return jnp.pad(shaped, ((0, 0), (0, 0), (0, PADQ - QUAD), (0, 0)))


def field_of(blocks):
    depth = blocks.shape[-1]
    shaped = blocks[:, :, :QUAD].reshape(4, 4, SHIFT, SHIFT, depth)
    return shaped.transpose(0, 2, 1, 3, 4).reshape(4 * SHIFT, 4 * SHIFT, depth)


def body(
    lats,
    lons,
    cells,
    cotangent,
    land,
    land_embed,
    qkv_weight,
    proj_weight,
    up_weight,
    down_weight,
    gain_one,
    gain_two,
):
    start = (
        cells.astype(F32) + land[:, :, None].astype(F32) * land_embed[None, None, :]
    ).astype(BF16)
    rows, hid = up_weight.shape
    width = cells.shape[2]
    deep = down_weight.shape[0]
    tokens = 4 * TOK
    rings = lons // 4
    first = lax.broadcasted_iota(jnp.int32, (rows, 128), 1) < 64
    shard_gain = jnp.where(first, gain_one[:, None], gain_two[:, None])

    def scatter_scratch(lines, across):
        quarter = across // 4
        return [
            pltpu.VMEM((rings, 2, lines, across), F32),
            pltpu.VMEM((rings, 2, lines, across), BF16),
            pltpu.VMEM((rings, 2, lines, across), BF16),
            pltpu.VMEM((3, rings, 2, lines, quarter), BF16),
            pltpu.VMEM((3, rings, 2, lines, quarter), BF16),
            pltpu.VMEM((rings, 2, lines, quarter), F32),
            pltpu.VMEM((rings - 1, 2, lines, quarter), BF16),
            pltpu.VMEM((rings - 1, 2, lines, quarter), BF16),
            pltpu.VMEM((2, lines, quarter), F32),
            pltpu.VMEM((4, 2, lines, quarter), F32),
            pltpu.VMEM((4, lines, quarter), F32),
        ]

    scratch = [
        pltpu.VMEM((4, 4, 2, PADQ, width), BF16),
        pltpu.VMEM((7, 2, PADQ, width), BF16),
        pltpu.VMEM((tokens + 16, width), F32),
        pltpu.VMEM((tokens + 16, width), F32),
        pltpu.VMEM((tokens, width), BF16),
        pltpu.VMEM((tokens, width), BF16),
        pltpu.VMEM((tokens, 3 * width), BF16),
        pltpu.VMEM((4 * HEADS, TOK, TOK), F32),
        pltpu.VMEM((tokens, width), BF16),
        pltpu.VMEM((tokens, width), F32),
        pltpu.VMEM((tokens + 16, width), F32),
        pltpu.VMEM((tokens, width), BF16),
        pltpu.VMEM((tokens, hid), BF16),
        pltpu.VMEM((tokens, hid), BF16),
        pltpu.VMEM((tokens, width), BF16),
        pltpu.VMEM((tokens, width), BF16),
        pltpu.VMEM((tokens, 3 * width), BF16),
        pltpu.VMEM((16, width), F32),
        pltpu.VMEM((16, width), F32),
        pltpu.VMEM((rows, 4 * width + 128), BF16),
        pltpu.VMEM((rings, 2, 2, rows, 4 * width + 128), BF16),
        pltpu.VMEM((rings, 2, 2, rows, hid), BF16),
        pltpu.VMEM((rings, 2, 2, deep, width), BF16),
    ]
    scratch += scatter_scratch(deep, width)
    scratch += scatter_scratch(rows, hid)
    for _ in range(5):
        scratch += scatter_scratch(rows, 2 * GROUP)
    wires = 14 + 14 + 3 * (3 * rings - 1) + 6 + 7 * (rings - 1 + 9) + 2 * rings + 5
    scratch += [pltpu.SemaphoreType.DMA((wires,)), pltpu.SemaphoreType.DMA((wires,))]
    vmem = pl.BlockSpec(memory_space=pltpu.VMEM)
    block_out, grad_cells, one, two, three = pl.pallas_call(
        functools.partial(kernel, lats, lons),
        out_shape=(
            jax.ShapeDtypeStruct((4, 4, PADQ, width), BF16),
            jax.ShapeDtypeStruct((4, 4, PADQ, width), BF16),
            jax.ShapeDtypeStruct((rows, 4 * width + 128), F32),
            jax.ShapeDtypeStruct((rows, hid), F32),
            jax.ShapeDtypeStruct((deep, width), F32),
        ),
        in_specs=[vmem] * 7,
        out_specs=(vmem,) * 5,
        scratch_shapes=scratch,
        compiler_params=pltpu.CompilerParams(
            collective_id=0, has_side_effects=True, vmem_limit_bytes=63 * 2**20
        ),
        name="block",
    )(
        blocks_of(start),
        blocks_of(cotangent),
        qkv_weight,
        proj_weight,
        shard_gain,
        up_weight,
        down_weight,
    )
    return (
        field_of(block_out),
        field_of(grad_cells),
        one[:, : 3 * width],
        one[:, 3 * width : 4 * width],
        two,
        three,
        one[:, 4 * width],
        one[:, 4 * width + 64],
    )


def solution(mesh):
    placed = (
        P("lat", "lon", None),
        P("lat", "lon", None),
        P("lat", "lon"),
        P(),
        P("lon", None),
        P("lon", None),
        P("lon", None),
        P("lon", None),
        P("lon"),
        P("lon"),
    )
    return jax.shard_map(
        functools.partial(body, mesh.shape["lat"], mesh.shape["lon"]),
        mesh=mesh,
        in_specs=placed,
        out_specs=(
            P("lat", "lon", None),
            P("lat", "lon", None),
            P("lon", None),
            P("lon", None),
            P("lon", None),
            P("lon", None),
            P("lon"),
            P("lon"),
        ),
        check_vma=False,
    )
```

```python
import functools

import jax
import jax.numpy as jnp
from jax import lax
from jax.experimental import pallas as pl
from jax.experimental.pallas import tpu as pltpu
from jax.sharding import PartitionSpec as P

HEADS = 16
WIN = 12
SHIFT = 6
EPS = 1e-5
NEG = -1e30
TOK = WIN * WIN
QUAD = SHIFT * SHIFT
PADQ = 48
GROUP = 256
F32 = jnp.float32
BF16 = jnp.bfloat16
MESH = pl.DeviceIdType.MESH


def nn(a, b):
    return lax.dot_general(a, b, (((1,), (0,)), ((), ())), preferred_element_type=F32)


def nt(a, b):
    return lax.dot_general(a, b, (((1,), (1,)), ((), ())), preferred_element_type=F32)


def tn(a, b):
    return lax.dot_general(a, b, (((0,), (0,)), ((), ())), preferred_element_type=F32)


def layer_norm(x):
    centred = x - jnp.mean(x, axis=-1, keepdims=True)
    spread = jnp.mean(centred * centred, axis=-1, keepdims=True)
    inverse = lax.rsqrt(spread + EPS)
    return centred * inverse, inverse


def norm_back(upstream, normed, inverse, gain):
    scaled = upstream * gain
    inner = (
        scaled
        - jnp.mean(scaled, axis=-1, keepdims=True)
        - normed * jnp.mean(scaled * normed, axis=-1, keepdims=True)
    )
    return inner * inverse, jnp.sum(upstream * normed, axis=0, keepdims=True)


class Marks:
    def __init__(self):
        self.open = None

    def __call__(self, name=None):
        if self.open is not None:
            self.open.__exit__(None, None, None)
        self.open = None
        if name is not None:
            self.open = jax.named_scope(name)
            self.open.__enter__()


class Place:
    def __init__(self, lats, lons):
        self.lats, self.lons, self.rings = lats, lons, lons // 4
        self.lat = lax.axis_index("lat")
        self.lon = lax.axis_index("lon")
        self.z = self.lon // 4
        self.yh = (self.lon // 2) % 2
        self.core = self.lon % 2
        self.sibling = (self.lat, self.lon + 1 - 2 * self.core)
        near = self.lat + 1 - 2 * (self.lat % 2)
        self.partner = (near, self.z * 4 + (1 - self.yh) * 2 + self.core)

        self.zs = [self.z] + [(self.z + by) % self.rings for by in range(1, self.rings)]
        side = self.yh * 2 + self.core
        self.on_z = [(self.lat, z * 4 + side) for z in self.zs]
        steps = ((0, 1), (1, 0), (1, 1))
        self.around = {}
        for by_lat, by_lon in steps:
            ahead = ((self.lat + by_lat) % lats, (self.lon + by_lon) % lons)
            behind = ((self.lat - by_lat + lats) % lats, (self.lon - by_lon + lons) % lons)
            self.around[by_lat, by_lon] = ahead
            self.around[-by_lat, -by_lon] = behind
        self.size = {"x": lats // 2, "y": 4}
        x, low = self.lat // 2, self.lat % 2
        xs = [x] + [(x + by) % (lats // 2) for by in range(1, lats // 2)]
        y = self.yh * 2 + low
        ys = [y] + [(y + by) % 4 for by in range(1, 4)]
        here = self.z * 4 + self.core
        self.on = {
            "x": [(number, (number * 2 + low, self.lon)) for number in xs],
            "y": [(number, (x * 2 + number % 2, here + number // 2 * 2)) for number in ys],
        }

    def z_of(self, by):
        return self.zs[by % self.rings]

    def along_z(self, by):
        return self.on_z[by % self.rings]

    def moved(self, by_lat, by_lon):
        return self.around[by_lat, by_lon]

    def at(self, axis, by):
        return self.on[axis][by % self.size[axis]]


class Wires:
    def __init__(self, send, recv):
        self.send, self.recv, self.used, self.sent = send, recv, 0, []

    def take(self, count):
        first = self.used
        self.used += count
        return first

    def copy(self, src, dst, index, device):
        return pltpu.make_async_remote_copy(
            src_ref=src,
            dst_ref=dst,
            send_sem=self.send.at[index],
            recv_sem=self.recv.at[index],
            device_id=device,
            device_id_type=MESH,
        )

    def start(self, src, dst, index, device, until=None):
        self.copy(src, dst, index, device).start()
        if until is not None:
            self.sent.append((until, index))

    def landed(self, ref, index, device):
        self.copy(ref, ref, index, device).wait_recv()

    def finish(self, device):
        for view, index in self.sent:
            ref = view()
            self.copy(ref, ref, index, device).wait_send()


class Gather:
    def __init__(self, place, wires, shard, whole):
        self.p, self.w, self.shard, self.whole = place, wires, shard, whole
        self.half = place.rings // 2
        self.last = 2 * self.half
        self.far = wires.take(1)
        self.way = {1: wires.take(self.last - 1), -1: wires.take(self.last - 1)}
        self.side = wires.take(place.rings)

    def slot(self, rel, other):
        p = self.p
        yh = 1 - p.yh if other else p.yh
        return self.whole.at[p.z_of(-rel), yh, p.core]

    def pair(self, rel, core):
        p = self.p
        return self.whole.at[p.z_of(-rel), :, core]

    def forward(self, way, hop, other):
        if hop == self.half - 1 and other != (way < 0):
            return
        index = self.way[way] + (2 * hop + other if hop < self.half - 1 else 2 * hop)
        block = self.slot(way * hop, other)
        self.w.start(block, block, index, self.p.along_z(way), lambda: self.whole.at[0, 0, 0])

    def landed(self, way, hop, other):
        index = self.way[way] + (2 * (hop - 1) + other if hop < self.half else 2 * (hop - 1))
        self.w.landed(self.slot(way * hop, other), index, self.p.along_z(-way))

    def share(self, rel):
        p = self.p
        index = self.side + rel % p.rings
        block = self.pair(rel, p.core)
        self.w.start(block, block, index, p.sibling, lambda: self.whole.at[0, :, 0])

    def tick(self, step):
        p = self.p
        if step == 0:
            here = self.slot(0, 0)
            here[...] = self.shard[...]
            for way in (1, -1):
                self.forward(way, 0, 0)
            self.w.start(self.shard, here, self.far, p.partner, lambda: self.shard)
        elif step == 1:
            self.w.landed(self.slot(0, 1), self.far, p.partner)
            for way in (1, -1):
                self.forward(way, 0, 1)
            self.share(0)
        elif step < self.last:
            hop, other = step // 2, step % 2
            for way in (1, -1):
                self.landed(way, hop, other)
                self.forward(way, hop, other)
            if other:
                for way in (1, -1):
                    self.share(way * hop)
        else:
            self.landed(1, self.half, 0)
            self.landed(-1, self.half, 1)
            self.share(self.half)

    def end(self):
        p = self.p
        for rel in range(p.rings):
            self.w.landed(self.pair(rel, 1 - p.core), self.side + rel, p.sibling)


class Quarters(Gather):
    def __init__(self, place, wires, shard, whole, axis):
        super().__init__(place, wires, shard, whole)
        self.axis = axis
        self.size = place.size[axis]
        self.count = shard.shape[1] // self.size
        self.over = wires.take(self.size - 1)
        self.mine = self.span(self.p.at(axis, 0)[0])
        partner = place.partner[0] % 2 + 2 * (1 - place.yh) if axis == "y" else place.lat // 2
        self.theirs = self.span(partner)

    def span(self, number):
        return pl.ds(pl.multiple_of(number * self.count, 128), self.count)

    def slot(self, rel, other):
        p = self.p
        yh = 1 - p.yh if other else p.yh
        return self.whole.at[p.z_of(-rel), yh, p.core, :, self.mine]

    def all_of(self, core, by):
        return self.whole.at[:, :, core, :, self.span(self.p.at(self.axis, by)[0])]

    def forward(self, way, hop, other):
        if hop == self.half - 1 and other != (way < 0):
            return
        index = self.way[way] + (2 * hop + other if hop < self.half - 1 else 2 * hop)
        block = self.slot(way * hop, other)
        self.w.start(block, block, index, self.p.along_z(way), lambda: self.slot(0, 0))

    def share(self, rel):
        pass

    def begin(self):
        p = self.p
        self.whole[p.z, p.yh, p.core, :, self.mine] = self.shard[:, self.mine]
        for way in (1, -1):
            self.forward(way, 0, 0)
        self.w.start(
            self.shard.at[:, self.theirs],
            self.whole.at[p.z, p.yh, p.core, :, self.theirs],
            self.far,
            p.partner,
            lambda: self.shard.at[:, self.mine],
        )

    def tick(self, step):
        if step == 0:
            self.begin()
        else:
            super().tick(step)

    def view(self):
        return self.all_of(self.p.core, 0)

    def exchange(self):
        block = self.view()
        self.w.start(block, block, self.side, self.p.sibling, self.view)
        for by in range(1, self.size):
            device = self.p.at(self.axis, by)[1]
            self.w.start(block, block, self.over + by - 1, device, self.view)

    def arrive(self):
        for by in range(1, self.size):
            block = self.all_of(self.p.core, -by)
            self.w.landed(block, self.over + by - 1, self.p.at(self.axis, -by)[1])
            self.w.start(block, block, self.side + by, self.p.sibling, self.view)

    def end(self):
        for by in range(self.size):
            self.w.landed(self.all_of(1 - self.p.core, -by), self.side + by, self.p.sibling)


class Scatter:
    def __init__(self, place, wires, refs, pieces, axis):
        self.p, self.w, self.pieces, self.axis = place, wires, pieces, axis
        self.own, self.away, self.near, self.give, self.got, self.sum = refs[:6]
        self.out, self.into, self.stage, self.land, self.full = refs[6:]
        self.size = place.size
        self.other = "y" if axis == "x" else "x"
        self.count = self.sum.shape[3]
        self.exchange = wires.take(pieces)
        self.over = wires.take(3)
        self.ring = wires.take(place.rings - 1)
        self.plane = wires.take(3)
        self.along = wires.take(3)

    def put(self, where, value):
        first, second = value[..., 0, :, :], value[..., 1, :, :]
        mine = self.p.core == 0
        self.own[where] = jnp.where(mine, first, second)
        self.away[where] = jnp.where(mine, second, first).astype(BF16)

    def trade(self, where, index):
        self.w.copy(
            self.away.at[where], self.near.at[where], self.exchange + index, self.p.sibling
        ).start()

    def traded(self, where, index):
        copy = self.w.copy(
            self.away.at[where], self.near.at[where], self.exchange + index, self.p.sibling
        )
        copy.wait_send()
        copy.wait_recv()

    def at(self, axis, by):
        return self.p.at(axis, by)

    def quarter(self, number):
        every = slice(None)
        first = pl.multiple_of(number * self.count, 128)
        at = (every, every, every, pl.ds(first, self.count))
        return self.own[at] + self.near[at].astype(F32)

    def cross(self):
        for by in range(1, self.size[self.axis]):
            number, device = self.at(self.axis, by)
            self.give[by - 1] = self.quarter(number).astype(BF16)
            source = self.give.at[by - 1]
            self.w.start(
                source, self.got.at[by - 1], self.over + by - 1, device, lambda: self.give.at[0]
            )

    def crossed(self):
        p = self.p
        total = self.quarter(self.at(self.axis, 0)[0])
        for by in range(1, self.size[self.axis]):
            device = self.at(self.axis, -by)[1]
            self.w.landed(self.got.at[by - 1], self.over + by - 1, device)
            total = total + self.got[by - 1].astype(F32)
        self.sum[...] = total
        for by in range(1, p.rings):
            self.out[by - 1] = self.sum[p.z_of(by)].astype(BF16)
            source = self.out.at[by - 1]
            self.w.start(
                source,
                self.into.at[by - 1],
                self.ring + by - 1,
                p.along_z(by),
                lambda: self.out.at[0],
            )

    def spread(self):
        p = self.p
        total = self.sum[p.z]
        for by in range(1, p.rings):
            self.w.landed(self.into.at[by - 1], self.ring + by - 1, p.along_z(-by))
            total = total + self.into[by - 1].astype(F32)
        self.stage[...] = total
        here = self.at(self.other, 0)[0]
        self.land[here] = self.stage[...]
        for by in range(1, self.size[self.other]):
            device = self.at(self.other, by)[1]
            self.w.start(
                self.stage,
                self.land.at[here],
                self.plane + by - 1,
                device,
                lambda: self.land.at[0],
            )

    def collect(self):
        p = self.p
        size = self.size[self.other]
        for by in range(1, size):
            number, device = self.at(self.other, -by)
            self.w.landed(self.land.at[number], self.plane + by - 1, device)
        total = self.land[0]
        for number in range(1, size):
            total = total + self.land[number]
        mine = self.at(self.other, 0)[0]
        self.land[mine] = total
        here = self.at(self.axis, 0)[0]
        self.full[here] = self.land[mine, p.yh]
        for by in range(1, self.size[self.axis]):
            number, device = self.at(self.axis, by)
            yh = p.yh if self.axis == "x" else number // 2
            self.w.start(
                self.land.at[mine, yh],
                self.full.at[here],
                self.along + by - 1,
                device,
                lambda: self.full.at[0],
            )

    def end(self):
        for by in range(1, self.size[self.axis]):
            number, device = self.at(self.axis, -by)
            self.w.landed(self.full.at[number], self.along + by - 1, device)

    def columns(self):
        return jnp.concatenate(
            [self.full[number] for number in range(self.size[self.axis])], axis=1
        )


def shifted_blocks():
    for window in range(4):
        for quarter in range(4):
            i = 2 * (window // 2) + quarter // 2
            j = 2 * (window % 2) + quarter % 2
            yield i, j, window, quarter, i == 3, j == 3


def kernel(
    lats,
    lons,
    cells_in,
    cotangent_in,
    qkv_shard,
    proj_shard,
    gain_shard,
    shard_two,
    shard_three,
    out_block,
    out_grad,
    out_one,
    out_two,
    out_three,
    moved,
    back,
    x_ref,
    up_ref,
    low_up,
    hidden_one,
    packed,
    probs_ref,
    attended,
    middle,
    result,
    hidden_two,
    active,
    grad_raised,
    grad_attended,
    grad_low,
    grad_packed,
    gains,
    sums,
    shard_one,
    one,
    two,
    three,
    *rest,
):
    scatter_refs, (send_sem, recv_sem) = rest[:-2], rest[-2:]
    p = Place(lats, lons)
    wires = Wires(send_sem, recv_sem)
    width = x_ref.shape[1]
    hid = shard_two.shape[1]
    chunk = hid // p.rings
    rows = width // lons
    tokens = 4 * TOK
    scale = (width // HEADS) ** -0.5
    per = GROUP * HEADS // width
    head = width // HEADS
    groups = width // GROUP

    mark = Marks()
    mark("barrier")
    shard_one[:, : 3 * width] = qkv_shard[...]
    shard_one[:, 3 * width : 4 * width] = proj_shard[...]
    shard_one[:, 4 * width :] = gain_shard[...]
    barrier = pltpu.get_barrier_semaphore()
    friends = [p.sibling] + [p.along_z(by) for by in range(1, p.rings)]
    friends += [p.at(axis, by)[1] for axis in ("x", "y") for by in range(1, p.size[axis])]
    for by_lat, by_lon in ((1, 0), (0, 1), (1, 1)):
        friends += [p.moved(by_lat, by_lon), p.moved(-by_lat, -by_lon)]
    for friend in friends:
        pl.semaphore_signal(barrier, inc=1, device_id=friend, device_id_type=MESH)
    pl.semaphore_wait(barrier, len(friends))

    def beyond(by_rows, by_columns, sign):
        return p.moved(sign * int(by_rows), sign * int(by_columns))

    mark("gather_one")
    halo = wires.take(14)
    fields, outs = (cells_in, cotangent_in), (out_block, out_grad)
    edge = [item for item in shifted_blocks() if item[4] or item[5]]
    first_weight = Gather(p, wires, shard_one, one)
    second_weight = Quarters(p, wires, shard_two, two, "x")
    third_weight = Quarters(p, wires, shard_three, three, "y")

    def send_halo(kind):
        for number, (i, j, window, quarter, down, over) in enumerate(edge):
            wires.start(
                fields[kind].at[(i + 1) % 4, (j + 1) % 4],
                moved.at[window, quarter, kind],
                halo + 7 * kind + number,
                beyond(down, over, -1),
                lambda: moved.at[0, 0, 0],
            )

    def assemble(kind, windows, target):
        numbers = {item[2:4]: number for number, item in enumerate(edge)}
        for i, j, window, quarter, down, over in shifted_blocks():
            if window not in windows:
                continue
            if down or over:
                wires.landed(
                    moved.at[window, quarter, kind],
                    halo + 7 * kind + numbers[(window, quarter)],
                    beyond(down, over, 1),
                )
                block = moved[window, quarter, kind]
            else:
                block = fields[kind][i + 1, j + 1]
            target[pl.ds(TOK * window + QUAD * quarter, PADQ)] = block.astype(F32)

    first_weight.tick(0)
    send_halo(0)
    second_weight.tick(0)
    third_weight.tick(0)
    for step in range(1, first_weight.last + 1):
        first_weight.tick(step)
        second_weight.tick(step)
        third_weight.tick(step)
    second_weight.exchange()
    third_weight.exchange()
    send_halo(1)
    mark("gather_one_end")
    first_weight.end()
    assemble(0, (0, 1, 2, 3), x_ref)

    def weight(ref, first, count):
        return ref[:, :, :, :, pl.ds(first, count)].reshape(width, count)

    mark("norm_one")
    turned = jnp.transpose(weight(one, 4 * width, 128).astype(F32), (1, 0))
    gains[0:8] = jnp.broadcast_to(turned[0:1], (8, width))
    gains[8:16] = jnp.broadcast_to(turned[64:65], (8, width))

    def by_rows(body):
        def run(window, _):
            body(pl.ds(pl.multiple_of(window * TOK, 16), TOK))
            return 0

        lax.fori_loop(0, 4, run, 0)

    def first_norm(at):
        normed, _ = layer_norm(x_ref[at])
        hidden_one[at] = (normed * gains[0:1]).astype(BF16)

    by_rows(first_norm)

    def columns(count, body):
        def run(number, _):
            body(pl.multiple_of(number * GROUP, GROUP), number)
            return 0

        lax.fori_loop(0, count, run, 0)

    def pack(first, number):
        packed[:, pl.ds(first, GROUP)] = nn(hidden_one[...], weight(one, first, GROUP)).astype(
            BF16
        )

    mark("qkv")
    columns(3 * groups, pack)

    mark("attend")
    lanes = lax.broadcasted_iota(jnp.int32, (TOK, GROUP), 1) // head
    late = lax.broadcasted_iota(jnp.int32, (TOK, TOK), 0) >= TOK // 2
    late_query = lax.broadcasted_iota(jnp.int32, (TOK, TOK), 1) >= TOK // 2
    differ = late != late_query

    def head_lanes(first):
        return pl.ds(pl.multiple_of(first, GROUP), GROUP)

    def at_turn(number, turns, turn_of):
        for turn in range(turn_of, len(turns), 2):
            if turns[turn]:

                def act(turn=turn):
                    for action in turns[turn]:
                        action()

                pl.when(number == turn // 2)(act)

    turns = [[] for _ in range(8 * groups)]
    turns[14].append(second_weight.arrive)
    turns[15].append(third_weight.arrive)

    def attend(number, _):
        window, group = number // groups, number % groups
        at = pl.ds(pl.multiple_of(window * TOK, 16), TOK)
        query = packed[at, head_lanes(group * GROUP)]
        keyed = packed[at, head_lanes(width + group * GROUP)]
        valued = packed[at, head_lanes(2 * width + group * GROUP)]
        split = jnp.logical_and(p.lat == lats - 1, window >= 2)
        bias = jnp.where(jnp.logical_and(differ, split), NEG, 0.0)
        value_turned = jnp.transpose(valued.astype(F32), (1, 0)).astype(BF16)
        parts = []
        for h in range(per):
            if h == per // 2:
                at_turn(number, turns, 0)
            mine = jnp.where(lanes == h, keyed, jnp.zeros_like(keyed))
            scores = nt(mine, query) * scale + bias
            raised = jnp.exp(scores - jnp.max(scores, axis=0, keepdims=True))
            probs = raised * (1.0 / jnp.sum(raised, axis=0, keepdims=True))
            probs_ref[number * per + h] = probs
            parts.append(nn(value_turned[h * head : (h + 1) * head], probs.astype(BF16)))
        attended[at, head_lanes(group * GROUP)] = jnp.transpose(
            jnp.concatenate(parts, axis=0), (1, 0)
        ).astype(BF16)
        at_turn(number, turns, 1)
        return 0

    lax.fori_loop(0, 4 * groups, attend, 0)
    mark("project")

    def project(first, number):
        middle[:, pl.ds(first, GROUP)] = x_ref[0:tokens, pl.ds(first, GROUP)] + nn(
            attended[...], weight(one, pl.multiple_of(3 * width + first, GROUP), GROUP)
        )

    columns(groups, project)
    assemble(1, (0, 1, 2, 3), up_ref)

    def second_norm(at):
        normed, _ = layer_norm(middle[at])
        hidden_two[at] = (normed * gains[8:9]).astype(BF16)
        low_up[at] = up_ref[at].astype(BF16)

    by_rows(second_norm)
    mark("gather_end")
    second_weight.end()
    third_weight.end()

    def scatter(number, pieces, axis):
        return Scatter(p, wires, scatter_refs[11 * number : 11 * number + 11], pieces, axis)

    scatter_down = scatter(0, p.rings, "y")
    scatter_up = scatter(1, p.rings, "x")
    scatter_proj = scatter(6, 1, "x")
    scatter_query = [scatter(2, 1, "y"), scatter(3, 1, "x")]
    scatter_value = [scatter(4, 1, "x"), scatter(5, 1, "y")]
    every = slice(None)

    def across(first, count):
        return (every, every, every, pl.ds(first, count))

    def ring_place(rel):
        return (p.z + rel + p.rings) % p.rings

    def feed(number, _):
        rel = jnp.where(
            number % 2 == 1, p.rings // 2 - (number + 1) // 2, p.rings // 2 + number // 2
        )
        place = ring_place(rel)
        first = pl.ds(pl.multiple_of(place * chunk, 128), chunk)
        up_weight = two[:, :, :, :, first].reshape(width, chunk)
        raised_up = nn(hidden_two[...], up_weight)
        share = 0.5 * (1.0 + lax.erf(raised_up * 0.7071067811865476))
        act = (raised_up * share).astype(BF16)
        active[:, first] = act
        slope = share + raised_up * jnp.exp(-0.5 * raised_up * raised_up) * 0.3989422804014327
        grad_down = tn(act, low_up[...])
        scatter_down.put((place,), grad_down.reshape(2, 2, chunk // 4, width))
        scatter_down.trade((place,), place)
        down_weight = three[place].reshape(chunk, width)
        grads = (nt(low_up[...], down_weight) * slope).astype(BF16)
        grad_raised[:, first] = grads
        grad_up = tn(hidden_two[...], grads)
        where = across(pl.multiple_of(place * chunk, 128), chunk)
        scatter_up.put(where, grad_up.reshape(p.rings, 2, 2, rows, chunk))
        scatter_up.trade(where, place)
        return 0

    mark("feed")
    lax.fori_loop(0, p.rings, feed, 0)

    def lower(first, number):
        down = three[:, :, :, :, pl.ds(first, GROUP)].reshape(hid, GROUP)
        result[0:tokens, pl.ds(first, GROUP)] = middle[:, pl.ds(first, GROUP)] + nn(
            active[...], down
        )

    def trade_all(number, _):
        scatter_down.traded((number,), number)
        scatter_up.traded(across(pl.multiple_of(number * chunk, 128), chunk), number)
        return 0

    mark("lower")
    columns(groups, lower)

    returns = wires.take(14)

    def send_back(source, kind):
        number = 0
        for i, j, window, quarter, down, over in shifted_blocks():
            first = TOK * window + QUAD * quarter
            block = source[pl.ds(first, PADQ)].astype(BF16)
            target = outs[kind].at[(i + 1) % 4, (j + 1) % 4]
            if down or over:
                place = back.at[number, kind]
                place[...] = block
                index = returns + 7 * kind + number
                wires.start(place, target, index, beyond(down, over, 1), lambda: back.at[0, 0])
                number += 1
            else:
                target[...] = block

    mark("return_out")
    send_back(result, 0)
    lax.fori_loop(0, p.rings, trade_all, 0)
    scatter_down.cross()
    scatter_up.cross()

    def raise_back(first, number):
        share = p.rings // groups
        up_rows = two[pl.ds(number * share, share)].reshape(GROUP, hid)
        result[0:tokens, pl.ds(first, GROUP)] = nt(grad_raised[...], up_rows)

    mark("raise_back")
    columns(groups, raise_back)

    sums[...] = jnp.zeros_like(sums)

    def second_back(at):
        normed, inverse = layer_norm(middle[at])
        through, total = norm_back(result[at], normed, inverse, gains[8:9])
        sums[8:16] += jnp.broadcast_to(total, (8, width))
        grad_middle = up_ref[at] + through
        up_ref[at] = grad_middle
        grad_low[at] = grad_middle.astype(BF16)

    mark("norm_two_back")
    by_rows(second_back)

    def split_columns(value):
        return value.reshape(p.rings, 2, 2, rows, value.shape[1])

    def project_back(first, number):
        grad = tn(attended[...], grad_low[:, pl.ds(first, GROUP)])
        scatter_proj.put(across(first, GROUP), split_columns(grad))
        share = p.rings // groups
        proj_rows = one[pl.ds(number * share, share), :, :, :, pl.ds(3 * width, width)]
        grad_attended[:, pl.ds(first, GROUP)] = nt(
            grad_low[...], proj_rows.reshape(GROUP, width)
        ).astype(BF16)

    mark("project_back")
    columns(groups, project_back)
    full = (every, every, every, every)
    scatter_proj.trade(full, 0)

    def attend_back(group, turns, number, _):
        window = number
        at = pl.ds(pl.multiple_of(window * TOK, 16), TOK)
        query = packed[at, head_lanes(group * GROUP)]
        keyed = packed[at, head_lanes(width + group * GROUP)]
        valued = packed[at, head_lanes(2 * width + group * GROUP)]
        upstream = grad_attended[at, head_lanes(group * GROUP)]
        key_turned = jnp.transpose(keyed.astype(F32), (1, 0)).astype(BF16)
        grad_key = jnp.zeros((TOK, GROUP), F32)
        grad_value = jnp.zeros((TOK, GROUP), F32)
        parts = []
        for h in range(per):
            if h == per // 2:
                at_turn(number, turns, 0)
            probs = probs_ref[(number * groups + group) * per + h]
            mine = lanes == h
            grad_probs = nt(jnp.where(mine, valued, jnp.zeros_like(valued)), upstream)
            grad_value = jnp.where(mine, nn(probs.astype(BF16), upstream), grad_value)
            inner = jnp.sum(grad_probs * probs, axis=0, keepdims=True)
            grad_scores = (probs * (grad_probs - inner) * scale).astype(BF16)
            grad_key = jnp.where(mine, nn(grad_scores, query), grad_key)
            parts.append(nn(key_turned[h * head : (h + 1) * head], grad_scores))
        grad_query = jnp.transpose(jnp.concatenate(parts, axis=0), (1, 0))
        grad_packed[at, head_lanes(group * GROUP)] = grad_query.astype(BF16)
        grad_packed[at, head_lanes(width + group * GROUP)] = grad_key.astype(BF16)
        grad_packed[at, head_lanes(2 * width + group * GROUP)] = grad_value.astype(BF16)
        at_turn(number, turns, 1)
        return 0

    def pack_back(group):
        def run(part, _):
            first = pl.multiple_of(part * width + group * GROUP, GROUP)
            grad = tn(hidden_one[...], grad_packed[:, pl.ds(first, GROUP)])
            where = across(pl.multiple_of(part * GROUP, GROUP), GROUP)
            scatter_query[group].put(where, split_columns(grad))
            return 0

        lax.fori_loop(0, 2, run, 0)
        scatter_query[group].trade(full, 0)
        first = 2 * width + group * GROUP
        grad = tn(hidden_one[...], grad_packed[:, first : first + GROUP])
        scatter_value[group].put(across(0, GROUP), split_columns(grad))

    def proj_cross():
        scatter_proj.traded(full, 0)
        scatter_proj.cross()

    def packed_cross(group):
        scatter_query[group].traded(full, 0)
        scatter_query[group].cross()
        scatter_value[group].traded(full, 0)
        scatter_value[group].cross()

    turns_one = [[] for _ in range(8)]
    turns_one[2].append(proj_cross)
    turns_two = [[] for _ in range(8)]
    turns_two[2].append(scatter_down.crossed)
    turns_two[4].append(scatter_up.crossed)
    turns_two[7].append(scatter_proj.crossed)
    turns_two[3].append(functools.partial(packed_cross, 0))

    mark("attend_back")
    lax.fori_loop(0, 4, functools.partial(attend_back, 0, turns_one), 0)
    mark("pack_back")
    pack_back(0)
    scatter_value[0].put(across(GROUP, GROUP), jnp.zeros((p.rings, 2, 2, rows, GROUP), F32))
    scatter_value[0].trade(full, 0)
    mark("attend_back_two")
    lax.fori_loop(0, 4, functools.partial(attend_back, 1, turns_two), 0)
    mark("pack_back_two")
    pack_back(1)
    for early in (scatter_query[0], scatter_value[0]):
        early.crossed()

    def unpack(first, number):
        share = p.rings // groups
        rows_here = one[pl.ds(number * share, share), :, :, :, pl.ds(0, 3 * width)]
        result[0:tokens, pl.ds(first, GROUP)] = nt(
            grad_packed[...], rows_here.reshape(GROUP, 3 * width)
        )

    columns(groups, unpack)
    scatter_down.spread()

    def first_back(at):
        normed, inverse = layer_norm(x_ref[at])
        through, total = norm_back(result[at], normed, inverse, gains[0:1])
        sums[0:8] += jnp.broadcast_to(total, (8, width))
        up_ref[at] = up_ref[at] + through

    mark("norm_one_back")
    by_rows(first_back)
    line = lax.broadcasted_iota(jnp.int32, (128, width), 0)
    both = jnp.where(line < 64, sums[0:1], sums[8:9])
    gain_sums = jnp.transpose(both, (1, 0))
    gain_sums = jnp.concatenate([gain_sums, gain_sums], axis=1)
    scatter_value[1].put(across(GROUP, GROUP), split_columns(gain_sums))
    mark("trade_last")
    scatter_value[1].trade(full, 0)
    scatter_query[1].traded(full, 0)
    scatter_query[1].cross()
    send_back(up_ref, 1)
    scatter_value[1].traded(full, 0)
    scatter_value[1].cross()
    mark("last")
    scatter_up.spread()
    scatter_proj.spread()
    scatter_down.collect()
    scatter_query[0].spread()
    scatter_value[0].spread()
    scatter_query[1].crossed()
    scatter_value[1].crossed()
    scatter_down.end()
    scatter_up.collect()
    scatter_proj.collect()
    scatter_query[0].collect()
    scatter_value[0].collect()
    scatter_query[1].spread()
    scatter_value[1].spread()
    scatter_up.end()
    scatter_proj.end()
    scatter_query[0].end()
    scatter_value[0].end()

    def write_packed(group):
        here = group * GROUP
        value = scatter_query[group].columns()
        out_one[:, here : here + GROUP] = value[:, :GROUP]
        out_one[:, width + here : width + here + GROUP] = value[:, GROUP:]
        value = scatter_value[group].columns()
        out_one[:, 2 * width + here : 2 * width + here + GROUP] = value[:, :GROUP]
        if group == 1:
            out_one[:, 4 * width :] = value[:, GROUP : GROUP + 128]

    out_three[...] = scatter_down.columns()
    out_two[...] = scatter_up.columns()
    out_one[:, 3 * width : 4 * width] = scatter_proj.columns()
    write_packed(0)
    mark("collect_last")
    scatter_query[1].collect()
    scatter_value[1].collect()
    number = 0
    for i, j, window, quarter, down, over in shifted_blocks():
        if down or over:
            for kind in range(2):
                wires.landed(
                    outs[kind].at[(i + 1) % 4, (j + 1) % 4],
                    returns + 7 * kind + number,
                    beyond(down, over, -1),
                )
            number += 1
    scatter_query[1].end()
    scatter_value[1].end()
    write_packed(1)
    mark("finish")
    wires.finish(p.sibling)
    mark()


def blocks_of(field):
    height, breadth, depth = field.shape
    shaped = field.reshape(height // SHIFT, SHIFT, breadth // SHIFT, SHIFT, depth)
    shaped = shaped.transpose(0, 2, 1, 3, 4).reshape(4, 4, QUAD, depth)
    return jnp.pad(shaped, ((0, 0), (0, 0), (0, PADQ - QUAD), (0, 0)))


def field_of(blocks):
    depth = blocks.shape[-1]
    shaped = blocks[:, :, :QUAD].reshape(4, 4, SHIFT, SHIFT, depth)
    return shaped.transpose(0, 2, 1, 3, 4).reshape(4 * SHIFT, 4 * SHIFT, depth)


def body(
    lats,
    lons,
    cells,
    cotangent,
    land,
    land_embed,
    qkv_weight,
    proj_weight,
    up_weight,
    down_weight,
    gain_one,
    gain_two,
):
    start = (
        cells.astype(F32) + land[:, :, None].astype(F32) * land_embed[None, None, :]
    ).astype(BF16)
    rows, hid = up_weight.shape
    width = cells.shape[2]
    deep = down_weight.shape[0]
    tokens = 4 * TOK
    rings = lons // 4
    first = lax.broadcasted_iota(jnp.int32, (rows, 128), 1) < 64
    shard_gain = jnp.where(first, gain_one[:, None], gain_two[:, None])

    def scatter_scratch(lines, across):
        quarter = across // 4
        return [
            pltpu.VMEM((rings, 2, lines, across), F32),
            pltpu.VMEM((rings, 2, lines, across), BF16),
            pltpu.VMEM((rings, 2, lines, across), BF16),
            pltpu.VMEM((3, rings, 2, lines, quarter), BF16),
            pltpu.VMEM((3, rings, 2, lines, quarter), BF16),
            pltpu.VMEM((rings, 2, lines, quarter), F32),
            pltpu.VMEM((rings - 1, 2, lines, quarter), BF16),
            pltpu.VMEM((rings - 1, 2, lines, quarter), BF16),
            pltpu.VMEM((2, lines, quarter), F32),
            pltpu.VMEM((4, 2, lines, quarter), F32),
            pltpu.VMEM((4, lines, quarter), F32),
        ]

    scratch = [
        pltpu.VMEM((4, 4, 2, PADQ, width), BF16),
        pltpu.VMEM((7, 2, PADQ, width), BF16),
        pltpu.VMEM((tokens + 16, width), F32),
        pltpu.VMEM((tokens + 16, width), F32),
        pltpu.VMEM((tokens, width), BF16),
        pltpu.VMEM((tokens, width), BF16),
        pltpu.VMEM((tokens, 3 * width), BF16),
        pltpu.VMEM((4 * HEADS, TOK, TOK), F32),
        pltpu.VMEM((tokens, width), BF16),
        pltpu.VMEM((tokens, width), F32),
        pltpu.VMEM((tokens + 16, width), F32),
        pltpu.VMEM((tokens, width), BF16),
        pltpu.VMEM((tokens, hid), BF16),
        pltpu.VMEM((tokens, hid), BF16),
        pltpu.VMEM((tokens, width), BF16),
        pltpu.VMEM((tokens, width), BF16),
        pltpu.VMEM((tokens, 3 * width), BF16),
        pltpu.VMEM((16, width), F32),
        pltpu.VMEM((16, width), F32),
        pltpu.VMEM((rows, 4 * width + 128), BF16),
        pltpu.VMEM((rings, 2, 2, rows, 4 * width + 128), BF16),
        pltpu.VMEM((rings, 2, 2, rows, hid), BF16),
        pltpu.VMEM((rings, 2, 2, deep, width), BF16),
    ]
    scratch += scatter_scratch(deep, width)
    scratch += scatter_scratch(rows, hid)
    for _ in range(5):
        scratch += scatter_scratch(rows, 2 * GROUP)
    wires = 14 + 14 + 3 * (3 * rings - 1) + 6 + 7 * (rings - 1 + 9) + 2 * rings + 5
    scratch += [pltpu.SemaphoreType.DMA((wires,)), pltpu.SemaphoreType.DMA((wires,))]
    vmem = pl.BlockSpec(memory_space=pltpu.VMEM)
    block_out, grad_cells, one, two, three = pl.pallas_call(
        functools.partial(kernel, lats, lons),
        out_shape=(
            jax.ShapeDtypeStruct((4, 4, PADQ, width), BF16),
            jax.ShapeDtypeStruct((4, 4, PADQ, width), BF16),
            jax.ShapeDtypeStruct((rows, 4 * width + 128), F32),
            jax.ShapeDtypeStruct((rows, hid), F32),
            jax.ShapeDtypeStruct((deep, width), F32),
        ),
        in_specs=[vmem] * 7,
        out_specs=(vmem,) * 5,
        scratch_shapes=scratch,
        compiler_params=pltpu.CompilerParams(
            collective_id=0, has_side_effects=True, vmem_limit_bytes=63 * 2**20
        ),
        name="block",
    )(
        blocks_of(start),
        blocks_of(cotangent),
        qkv_weight,
        proj_weight,
        shard_gain,
        up_weight,
        down_weight,
    )
    return (
        field_of(block_out),
        field_of(grad_cells),
        one[:, : 3 * width],
        one[:, 3 * width : 4 * width],
        two,
        three,
        one[:, 4 * width],
        one[:, 4 * width + 64],
    )


def solution(mesh):
    placed = (
        P("lat", "lon", None),
        P("lat", "lon", None),
        P("lat", "lon"),
        P(),
        P("lon", None),
        P("lon", None),
        P("lon", None),
        P("lon", None),
        P("lon"),
        P("lon"),
    )
    return jax.shard_map(
        functools.partial(body, mesh.shape["lat"], mesh.shape["lon"]),
        mesh=mesh,
        in_specs=placed,
        out_specs=(
            P("lat", "lon", None),
            P("lat", "lon", None),
            P("lon", None),
            P("lon", None),
            P("lon", None),
            P("lon", None),
            P("lon"),
            P("lon"),
        ),
        check_vma=False,
    )
```
